256 devices in a mesh: dp: 16 (over z, y_hi), seq: 16 (over y_lo, x, core).
Axes of the slice: x: 4, y: 4 (y_hi: 2, y_lo: 2; y = y_hi * 2 + y_lo), z: 8, core: 2. Of those that a mesh axis runs over, the one named last changes fastest.
Arguments:
- q_proj: bfloat16 [32, 2048, 4096], P('dp', 'seq'), may hold values from -6 to 6
- k_proj: bfloat16 [32, 2048, 1024], P('dp', 'seq'), may hold values from -6 to 6
- v_proj: bfloat16 [32, 2048, 1024], P('dp', 'seq'), may hold values from -6 to 6
- hidden_in: bfloat16 [32, 2048, 4096], P('dp', 'seq'), may hold values from -6 to 6
- out_weight: bfloat16 [4096, 4096], P('seq'), may hold values from -0.09375 to 0.09375
- doc_lengths: int32 [32], P('dp'), may hold values from 512 to 2048, as said below
- positive: int32 [32], replicated, may hold values from 0 to 31, as said below
Outputs:
- passage_contrast_cost: float32 [32], P('dp')
- wo_grad: float32 [4096, 4096], P('seq', 'dp')
The draws below stay inside these ranges and needn't reach their ends.
Inputs may be any that keep to these rules, and one draw needn't show every extreme that they name: `doc_lengths`: some document has exactly 2048 valid positions. `positive`: never the document itself.
All inputs are finite; a program needn't handle non-finite values.
Results may differ from the reference program's by a relative error of at most 0.00055.
Values may be sent and summed in bfloat16 or wider, within the bound.
A program may use at most 128 MiB of HBM per device.

```python
import math
import jax
import jax.numpy as jnp
from jax import lax

D = 4096
QUERY_HEADS = 32
KEY_VALUE_HEADS = 8
HEAD_SIZE = 128
QW = 4096
KW = 1024
LEN = 2048
DOCS = 32


def draw_q_proj(key, part):
    key = jax.random.fold_in(key, 1)
    result = jnp.clip(jax.random.normal(key, (DOCS, LEN, QW), jnp.float32), -6.0, 6.0)
    return result.astype(jnp.bfloat16)


def draw_k_proj(key, part):
    key = jax.random.fold_in(key, 2)
    result = jnp.clip(jax.random.normal(key, (DOCS, LEN, KW), jnp.float32), -6.0, 6.0)
    return result.astype(jnp.bfloat16)


def draw_doc_lengths(key, part):
    key = jax.random.fold_in(key, 3)
    drawn = jax.random.randint(key, (DOCS,), LEN // 4, LEN + 1)
    return jnp.where(jnp.arange(DOCS) == 0, LEN, drawn).astype(jnp.int32)


def draw_positive(key, part):
    key = jax.random.fold_in(key, 4)
    offsets = jax.random.randint(key, (DOCS,), 1, DOCS)
    return ((jnp.arange(DOCS) + offsets) % DOCS).astype(jnp.int32)


def block_scale(rng, shape, shards, low, largest):
    factor_of = 1.0
    for axis_at, shards_of in shards:
        draws = jax.random.uniform(jax.random.fold_in(jax.random.fold_in(rng, 6), axis_at), (shards_of,), jnp.float32, low / len(shards), largest / len(shards))
        factor_of = factor_of * jnp.repeat(jnp.exp(draws), shape[axis_at] // shards_of).reshape((-1,) + (1,) * (len(shape) - 1 - axis_at))
    return factor_of


def centred(rng, extent, spread, reach, shards=(), kind=jnp.bfloat16):
    factor_of = block_scale(rng, extent, shards, -0.22, 0.18) if shards else 1.0
    values = jax.random.normal(rng, extent, jnp.float32) * spread * factor_of
    return jnp.minimum(jnp.maximum(values, -reach), reach).astype(kind)


def setup_inputs(seed: int = 0) -> dict:
    keys = jax.random.split(jax.random.key(seed), 8)
    return {
        "q_proj": draw_q_proj(jax.random.fold_in(keys[7], 71), 0),
        "k_proj": draw_k_proj(jax.random.fold_in(keys[7], 71), 0),
        "v_proj": centred(keys[2], (DOCS, LEN, KW), 1.0, 6.0, ((0, 16), (1, 16))),
        "hidden_in": centred(keys[3], (DOCS, LEN, D), 1.0, 6.0, ((0, 16), (1, 16))),
        "out_weight": centred(keys[4], (QW, D), QW ** -0.5, 0.09375, ((0, 16),)),
        "doc_lengths": draw_doc_lengths(jax.random.fold_in(keys[7], 71), 0),
        "positive": draw_positive(jax.random.fold_in(keys[7], 71), 0),
    }


logit_divisor = 0.05
norm_eps = 1e-06

def attend_doc(inputs):
    rows_of_query, rows_of_key, rows_of_value = inputs
    sequence_length = rows_of_query.shape[0]
    block_rows = min(512, sequence_length)
    head_groups = QUERY_HEADS // KEY_VALUE_HEADS
    heads_of_query = rows_of_query.reshape(sequence_length, KEY_VALUE_HEADS, head_groups, HEAD_SIZE).astype(jnp.float32)
    heads_of_key = rows_of_key.reshape(sequence_length, KEY_VALUE_HEADS, HEAD_SIZE).astype(jnp.float32)
    heads_of_value = rows_of_value.reshape(sequence_length, KEY_VALUE_HEADS, HEAD_SIZE).astype(jnp.float32)
    outputs = []
    for block_index in range(sequence_length // block_rows):
        row_start = block_index * block_rows
        row_stop = row_start + block_rows
        scores = jnp.einsum('qhgd,khd->hgqk', heads_of_query[row_start:row_stop], heads_of_key[:row_stop]) / math.sqrt(HEAD_SIZE)
        visible = jnp.arange(row_start, row_stop)[:, None] >= jnp.arange(row_stop)[None, :]
        scores = jnp.where(visible, scores, -1e+30)
        row_peak = lax.optimization_barrier(jnp.max(scores, axis=-1, keepdims=True))
        raised_logits = jnp.exp(scores - row_peak)
        cumulative_sums = lax.optimization_barrier(jnp.sum(raised_logits, axis=-1, keepdims=True))
        rounded = lax.optimization_barrier(raised_logits.astype(jnp.bfloat16)).astype(jnp.float32)
        mixed_out = jnp.einsum('hgqk,khd->hgqd', rounded, heads_of_value[:row_stop]) / cumulative_sums
        mixed_out = jnp.transpose(mixed_out, (2, 0, 1, 3)).reshape(block_rows, QUERY_HEADS * HEAD_SIZE)
        outputs.append(mixed_out.astype(jnp.bfloat16))
    return jnp.concatenate(outputs, 0)

def contrast(source_pooled, full_pooled_matrix, targets, row_first):
    passage_similarities = jnp.dot(source_pooled, full_pooled_matrix.T, precision=lax.Precision.HIGHEST) / logit_divisor
    target_slot = jnp.arange(full_pooled_matrix.shape[0])[None, :]
    source_slot = row_first + jnp.arange(source_pooled.shape[0])[:, None]
    raised_logits = jnp.exp(passage_similarities - 1.0 / logit_divisor) * (target_slot != source_slot).astype(jnp.float32)
    cumulative_sums = lax.optimization_barrier(jnp.sum(raised_logits, axis=1, keepdims=True))
    chosen_entries = (target_slot == targets[:, None]).astype(jnp.float32)
    passage_contrast_cost = jnp.log(cumulative_sums[:, 0]) + 1.0 / logit_divisor - lax.optimization_barrier(jnp.sum(passage_similarities * chosen_entries, axis=1))
    return (passage_contrast_cost, raised_logits / cumulative_sums - chosen_entries)

def reference(q_proj, k_proj, v_proj, hidden_in, out_weight, doc_lengths, positive):
    attended = lax.map(attend_doc, (q_proj, k_proj, v_proj))
    valid_rows = (jnp.arange(LEN)[None, :] < doc_lengths[:, None]).astype(jnp.float32)
    counts = doc_lengths.astype(jnp.float32)[:, None]
    pooled = jnp.einsum('dt,dtc->dc', valid_rows, attended.astype(jnp.float32)) / counts
    residual = jnp.einsum('dt,dtc->dc', valid_rows, hidden_in.astype(jnp.float32)) / counts
    raw_embed = residual + jnp.dot(pooled, out_weight.astype(jnp.float32), precision=lax.Precision.HIGHEST)
    squares = lax.optimization_barrier(jnp.sum(raw_embed * raw_embed, axis=1, keepdims=True)) + norm_eps
    inv_norm = lax.rsqrt(squares)
    unit_embed = raw_embed * inv_norm
    passage_contrast_cost, grad_sims = contrast(unit_embed, unit_embed, positive, 0)
    source_slice = jnp.dot(grad_sims, unit_embed, precision=lax.Precision.HIGHEST)
    target_slice = jnp.dot(grad_sims.T, unit_embed, precision=lax.Precision.HIGHEST)
    pooled_derivative = (source_slice + target_slice) / logit_divisor
    along_grad = lax.optimization_barrier(jnp.sum(raw_embed * pooled_derivative, axis=1, keepdims=True))
    grad_raw = (pooled_derivative - raw_embed * along_grad / squares) * inv_norm
    wo_grad = jnp.dot(pooled.T, grad_raw, precision=lax.Precision.HIGHEST)
    return (passage_contrast_cost, wo_grad)
```

```python
import math

import jax
import jax.numpy as jnp
from jax import lax
from jax.experimental import pallas as pl
from jax.experimental.pallas import tpu as pltpu
from jax.sharding import PartitionSpec as P

MESH = pl.DeviceIdType.MESH
F32 = jnp.float32
BF16 = jnp.bfloat16
HIGHEST = lax.Precision.HIGHEST
LANES = 128
TOK = 128
RANKS = 16
HEADS = 4
LEN = 2048
QB = 256
EXP2_SCALE = math.log2(math.e) / math.sqrt(128.0)
INV_TEMP = 20.0
EPS = 1e-06

(K_SEM, Q_SEM, V_SEM, SIB_SEM, RS_SEM, RG_SEM, TG_SEM, PG_SEM, GRAM_SEM, HID_SEM, W_SEM) = (
    0, 1, 5, 6, 7, 8, 9, 10, 11, 12, 13)
N_SEM = 14


def split3(x):
    hi = x.astype(BF16).astype(F32)
    mid = (x - hi).astype(BF16).astype(F32)
    lo = x - hi - mid
    return hi, mid, lo


def kernel(
    q_ref, k_ref, v_ref, hid_ref, wt_ref, len_ref, pos_ref,
    cost_ref, wo_ref,
    qbuf, kbuf, vbuf, hbuf, wbuf, sbuf, wsum, resid,
    sib, rs_out, rs_buf, rtile, rg_buf, tg_buf, ptile, pg_buf, gtile, gram_buf,
    lhs_ref, rt_mat, pa_mat, rg_mat,
    send_sem, recv_sem,
):
    g = lax.axis_index("dp")
    s = lax.axis_index("seq")
    core = s % 2
    col = (s // 2) % 4
    row = s // 8

    def seq_peer(e):
        odd = e % 2
        i = (e // 2) % 4
        dc = 1 - e // 8
        dx = (i + 3 - 2 * odd) % 4
        return ((row + 1 - odd) % 2) * 8 + ((col + dx) % 4) * 2 + (core + dc) % 2

    hid_copy = pltpu.make_async_copy(hid_ref, hbuf, recv_sem.at[HID_SEM])
    hid_copy.start()
    wt_copy = pltpu.make_async_copy(wt_ref, wbuf, recv_sem.at[W_SEM])
    wt_copy.start()

    barrier = pltpu.get_barrier_semaphore()

    def greet(e, c):
        @pl.when(e < RANKS - 1)
        def _():
            pl.semaphore_signal(barrier, inc=1, device_id=(g, seq_peer(e)), device_id_type=MESH)
            pl.semaphore_signal(
                barrier, inc=1, device_id=((g + e + 1) % RANKS, s), device_id_type=MESH)

        @pl.when(jnp.logical_or(s != g, e != g))
        def _():
            pl.semaphore_signal(barrier, inc=1, device_id=(e, g), device_id_type=MESH)

        return c

    lax.fori_loop(0, RANKS, greet, 0)
    pl.semaphore_wait(barrier, 2 * (RANKS - 1) + RANKS - jnp.where(s == g, 1, 0))

    def remote(src, dst, sem, target):
        pltpu.make_async_remote_copy(
            src_ref=src, dst_ref=dst, send_sem=send_sem.at[sem], recv_sem=recv_sem.at[sem],
            device_id=target, device_id_type=MESH,
        ).start()

    def cols(first):
        return pl.ds(pl.multiple_of(first * LANES, LANES), LANES)

    def send_k(e, c):
        t = seq_peer(e)
        remote(k_ref.at[t % 2, :, cols(t // 2)], kbuf.at[s], K_SEM, (g, t))
        return c

    def send_q(h):
        def body(e, c):
            t = seq_peer(e)
            remote(q_ref.at[t % 2, :, cols((t // 2) * HEADS + h)], qbuf.at[h, s], Q_SEM + h, (g, t))
            return c
        return body

    def send_v(e, c):
        t = seq_peer(e)
        remote(v_ref.at[t % 2, :, cols(t // 2)], vbuf.at[s], V_SEM, (g, t))
        return c

    pltpu.make_async_copy(k_ref.at[core, :, cols(s // 2)], kbuf.at[s], recv_sem.at[K_SEM]).start()
    lax.fori_loop(0, RANKS - 1, send_k, 0)

    def send_head(h, c):
        pltpu.make_async_copy(
            q_ref.at[core, :, cols((s // 2) * HEADS + h)], qbuf.at[h, s], recv_sem.at[Q_SEM + h]
        ).start()
        lax.fori_loop(0, RANKS - 1, send_q(h), 0)
        return c

    lax.fori_loop(0, HEADS, send_head, 0)
    pltpu.make_async_copy(v_ref.at[core, :, cols(s // 2)], vbuf.at[s], recv_sem.at[V_SEM]).start()
    lax.fori_loop(0, RANKS - 1, send_v, 0)

    def wait_all(ref, sem):
        pltpu.make_async_copy(ref, ref, sem).wait()

    len0 = len_ref[0]
    len1 = len_ref[1]

    hid_copy.wait()
    place = s * TOK + lax.broadcasted_iota(jnp.int32, (16, TOK), 1)
    ones = jnp.ones((16, TOK), F32)
    zeros = jnp.zeros((16, TOK), F32)
    for doc, length in ((0, len0), (1, len1)):
        mask = jnp.where(place < length, ones, zeros).astype(BF16)
        inv_len = jnp.full((1, 1), 1.0, F32) / jnp.full((1, 1), length, jnp.int32).astype(F32)

        def add_resid(t, c, doc=doc, mask=mask, inv_len=inv_len):
            part = jnp.dot(
                mask, hbuf[doc, :, pl.ds(pl.multiple_of(t * 256, 256), 256)],
                preferred_element_type=F32) * inv_len
            resid[t, doc:doc + 1, :] = part[0:1, 0:LANES]
            resid[t, 2 + doc:3 + doc, :] = part[0:1, LANES:]
            return c

        lax.fori_loop(0, RANKS, add_resid, 0)

    my_len = len_ref[core]

    wait_all(kbuf, recv_sem.at[K_SEM])

    def one_head(h, c):
        wait_all(qbuf.at[h], recv_sem.at[Q_SEM + h])
        for i in range(LEN // QB):
            n = (i + 1) * QB
            nb = n // TOK
            keys = kbuf[0:nb].reshape(n, LANES)
            queries = qbuf[h, 2 * i:2 * i + 2].reshape(QB, LANES)
            sref = sbuf.at[i % 2]
            sref[0:n, :] = lax.dot_general(
                keys, queries, (((1,), (1,)), ((), ())), preferred_element_type=F32)
            diag = sref[n - QB:n, :]
            vis = lax.broadcasted_iota(jnp.int32, (QB, QB), 0) <= lax.broadcasted_iota(
                jnp.int32, (QB, QB), 1)
            sref[n - QB:n, :] = jnp.where(vis, diag, -1e30)
            peak = sref[0:8, :]
            for r in range(8, n, 8):
                peak = jnp.maximum(peak, sref[r:r + 8, :])
            peak = jnp.max(peak, axis=0, keepdims=True)
            total = jnp.zeros((8, QB), F32)
            step = 64
            for r in range(0, n, step):
                e = jnp.exp2((sref[r:r + step, :] - peak) * EXP2_SCALE)
                sref[r:r + step, :] = e
                total = total + jnp.sum(e.reshape(step // 8, 8, QB), axis=0)
            total = jnp.sum(total, axis=0, keepdims=True)
            t_at = i * QB + lax.broadcasted_iota(jnp.int32, (1, QB), 1)
            ratio = jnp.where(t_at < my_len, 1.0 / total, 0.0)
            for r in range(0, n, step):
                e = sref[r:r + step, :] * ratio
                e = e[:, 0:LANES] + e[:, LANES:]
                if r >= n - QB:
                    wsum[r:r + step, :] = e
                else:
                    wsum[r:r + step, :] += e
        lane_ones = jnp.ones((8, LANES), F32)
        w_row = lax.dot_general(
            lane_ones, wsum[...], (((1,), (1,)), ((), ())), precision=HIGHEST,
            preferred_element_type=F32)
        lhs_ref[h] = w_row
        return c

    lax.fori_loop(0, HEADS, one_head, 0)

    wait_all(vbuf, recv_sem.at[V_SEM])
    inv_my_len = jnp.full((1, 1), 1.0, F32) / jnp.full((1, 1), my_len, jnp.int32).astype(F32)
    parts = [split3(lhs_ref[h, 0:1, :]) for h in range(HEADS)]
    lhs = jnp.concatenate(
        [parts[h][p] for p in range(3) for h in range(HEADS)]
        + [jnp.zeros((4, LEN), F32)], axis=0).astype(BF16)
    out = jnp.dot(lhs, vbuf[...].reshape(LEN, LANES), preferred_element_type=F32)
    mine = (out[0:4] + out[4:8] + out[8:12]) * inv_my_len
    mine = jnp.concatenate([mine, jnp.zeros((4, LANES), F32)], axis=0)

    @pl.when(core == 0)
    def _():
        sib[0] = mine
        remote(sib.at[0], sib.at[0], SIB_SEM, (g, s + 1))

    @pl.when(core == 1)
    def _():
        sib[1] = mine
        remote(sib.at[1], sib.at[1], SIB_SEM, (g, s - 1))

    wait_all(sib.at[0], recv_sem.at[SIB_SEM])
    low = core == 0
    doc0 = jnp.where(low, sib[0, 0:2, :], sib[0, 2:4, :])
    doc1 = jnp.where(low, sib[1, 0:2, :], sib[1, 2:4, :])
    both = jnp.concatenate(
        [doc0[0:1], doc1[0:1], doc0[1:2], doc1[1:2], jnp.zeros((4, LANES), F32)], axis=0)
    ptile[...] = both
    pg_buf[g] = both

    pooled = jnp.concatenate([both[0:2], both[2:4]], axis=1)
    hi, mid, lo = split3(pooled)
    lhs2 = jnp.concatenate([hi, mid, lo, jnp.zeros((10, 2 * LANES), F32)], axis=0).astype(BF16)

    wt_copy.wait()

    def project(e, c):
        t = seq_peer(e)
        part = jnp.dot(
            lhs2, wbuf[:, pl.ds(pl.multiple_of(t * 256, 256), 256)], preferred_element_type=F32)
        part = part[0:2] + part[2:4] + part[4:6]
        tile = resid[t]
        tile = jnp.concatenate(
            [tile[0:2] + part[:, 0:LANES], tile[2:4] + part[:, LANES:],
             jnp.zeros((4, LANES), F32)], axis=0)

        @pl.when(e < RANKS - 1)
        def _():
            rs_out[e] = tile
            remote(rs_out.at[e], rs_buf.at[s], RS_SEM, (g, t))

        @pl.when(e == RANKS - 1)
        def _():
            rs_buf[s] = tile

        return c

    lax.fori_loop(0, RANKS, project, 0)

    def send_pooled(e, c):
        remote(ptile, pg_buf.at[g], PG_SEM, ((g + e + 1) % RANKS, s))
        return c

    lax.fori_loop(0, RANKS - 1, send_pooled, 0)

    wait_all(rs_buf.at[pl.ds(0, RANKS - 1)], recv_sem.at[RS_SEM])
    raw = jnp.sum(rs_buf[...], axis=0)
    rtile[...] = raw
    rg_buf[g] = raw

    def send_raw(e, c):
        remote(rtile, rg_buf.at[g], RG_SEM, ((g + e + 1) % RANKS, s))
        return c

    lax.fori_loop(0, RANKS - 1, send_raw, 0)

    @pl.when(s == g)
    def _():
        tg_buf[g] = raw

    def send_cols(e, c):
        @pl.when(jnp.logical_or(s != g, e != s))
        def _():
            remote(rtile, tg_buf.at[g], TG_SEM, (s, e))
        return c

    lax.fori_loop(0, RANKS, send_cols, 0)

    wait_all(rg_buf.at[pl.ds(0, RANKS - 1)], recv_sem.at[RG_SEM])
    for d in range(RANKS):
        for half in range(2):
            piece = rg_buf[d, 2 * half:2 * half + 2, :]
            for rep in range(4):
                rg_mat[32 * rep + 2 * d:32 * rep + 2 * d + 2, half * LANES:(half + 1) * LANES] = piece
    wide = lax.dot_general(
        rg_mat[0:32, :], rg_mat[...], (((1,), (1,)), ((), ())), precision=HIGHEST,
        preferred_element_type=F32)
    lane_group = lax.broadcasted_iota(jnp.int32, (8, LANES), 1) // 32
    packed = jnp.zeros((8, LANES), F32)
    for p in range(4):
        packed = packed + jnp.where(lane_group == p, wide[8 * p:8 * p + 8], 0.0)
    gtile[...] = packed
    gram_buf[s] = packed

    def send_gram(e, c):
        remote(gtile, gram_buf.at[s], GRAM_SEM, (g, seq_peer(e)))
        return c

    lax.fori_loop(0, RANKS - 1, send_gram, 0)

    wait_all(pg_buf.at[pl.ds(0, RANKS - 1)], recv_sem.at[PG_SEM])
    for d in range(RANKS):
        for half in range(2):
            pa_mat[2 * d:2 * d + 2, half * LANES:(half + 1) * LANES] = pg_buf[
                d, 2 * half:2 * half + 2, :]

    @pl.when(s == g)
    def _():
        wait_all(tg_buf.at[pl.ds(0, RANKS - 1)], recv_sem.at[TG_SEM])

    @pl.when(s != g)
    def _():
        wait_all(tg_buf, recv_sem.at[TG_SEM])

    for d in range(RANKS):
        for half in range(2):
            rt_mat[2 * d:2 * d + 2, half * LANES:(half + 1) * LANES] = tg_buf[
                d, 2 * half:2 * half + 2, :]

    wait_all(gram_buf.at[pl.ds(0, RANKS - 1)], recv_sem.at[GRAM_SEM])
    gp = jnp.sum(gram_buf[...], axis=0)
    gram = jnp.concatenate(
        [gp if p == 0 else pltpu.roll(gp, LANES - 32 * p, 1) for p in range(4)], axis=0)
    ri = lax.broadcasted_iota(jnp.int32, (32, LANES), 0)
    ci = lax.broadcasted_iota(jnp.int32, (32, LANES), 1)
    inside = ci < 32
    eye = ri == ci
    gram = jnp.where(inside, gram, 0.0)
    on_diag = jnp.where(eye, gram, 0.0)
    sq_i = jnp.sum(on_diag, axis=1, keepdims=True) + EPS
    sq_j = jnp.sum(on_diag, axis=0, keepdims=True) + EPS
    inv_i = lax.rsqrt(sq_i)
    inv_j = lax.rsqrt(sq_j)
    sims = gram * inv_i * inv_j * INV_TEMP
    raised = jnp.where(jnp.logical_and(inside, jnp.logical_not(eye)), jnp.exp(sims - INV_TEMP), 0.0)
    tot_i = jnp.sum(raised, axis=1, keepdims=True)
    tot_j = jnp.sum(raised, axis=0, keepdims=True)
    tot_j = jnp.where(ci[0:1] < 32, tot_j, 1.0)
    hot_t = jnp.where(jnp.logical_and(ri == pos_ref[...], inside), 1.0, 0.0)
    eye_f = jnp.where(eye, 1.0, 0.0)
    hot = lax.dot_general(
        jnp.where(lax.broadcasted_iota(jnp.int32, (32, LANES), 0)
                  == lax.broadcasted_iota(jnp.int32, (32, LANES), 1), 1.0, 0.0),
        jnp.concatenate([hot_t, jnp.zeros((96, LANES), F32)], axis=0),
        (((1,), (1,)), ((), ())), precision=HIGHEST, preferred_element_type=F32)
    cost = jnp.log(tot_i) + INV_TEMP - jnp.sum(sims * hot, axis=1, keepdims=True)
    both_grad = raised / tot_i + raised / tot_j - hot - hot_t
    weighted = both_grad * inv_j * INV_TEMP
    along = jnp.sum(weighted * gram, axis=1, keepdims=True)
    coef = inv_i * weighted - eye_f * (inv_i * along / sq_i)
    grad_raw = jnp.dot(coef[:, 0:32], rt_mat[...], precision=HIGHEST, preferred_element_type=F32)
    wo_ref[...] = lax.dot_general(
        pa_mat[...], grad_raw, (((0,), (0,)), ((), ())), precision=HIGHEST,
        preferred_element_type=F32)
    doc_at = lax.broadcasted_iota(jnp.int32, (32, 1), 0)
    cost_ref[0] = jnp.sum(jnp.where(doc_at == 2 * g, cost, 0.0))
    cost_ref[1] = jnp.sum(jnp.where(doc_at == 2 * g + 1, cost, 0.0))

    some = RANKS - 1
    wait_all(kbuf.at[pl.ds(0, some)], send_sem.at[K_SEM])
    for h in range(HEADS):
        wait_all(qbuf.at[h, pl.ds(0, some)], send_sem.at[Q_SEM + h])
    wait_all(vbuf.at[pl.ds(0, some)], send_sem.at[V_SEM])
    wait_all(sib.at[0], send_sem.at[SIB_SEM])
    wait_all(rs_buf.at[pl.ds(0, some)], send_sem.at[RS_SEM])
    wait_all(rg_buf.at[pl.ds(0, some)], send_sem.at[RG_SEM])

    @pl.when(s == g)
    def _():
        wait_all(tg_buf.at[pl.ds(0, some)], send_sem.at[TG_SEM])

    @pl.when(s != g)
    def _():
        wait_all(tg_buf, send_sem.at[TG_SEM])

    wait_all(pg_buf.at[pl.ds(0, some)], send_sem.at[PG_SEM])
    wait_all(gram_buf.at[pl.ds(0, some)], send_sem.at[GRAM_SEM])


def shards(q_proj, k_proj, v_proj, hidden_in, out_weight, doc_lengths, positive):
    any_spec = pl.BlockSpec(memory_space=pl.ANY)
    smem = pl.BlockSpec(memory_space=pltpu.SMEM)
    vmem = pl.BlockSpec(memory_space=pltpu.VMEM)
    wide_pos = jnp.pad(positive.reshape(1, 32), ((0, 0), (0, LANES - 32)))
    tile = (RANKS, 8, LANES)
    return pl.pallas_call(
        kernel,
        out_shape=(
            jax.ShapeDtypeStruct((2,), F32),
            jax.ShapeDtypeStruct((256, 256), F32),
        ),
        in_specs=[any_spec] * 5 + [smem, vmem],
        out_specs=(smem, vmem),
        scratch_shapes=[
            pltpu.VMEM((HEADS, RANKS, TOK, LANES), BF16),
            pltpu.VMEM((RANKS, TOK, LANES), BF16),
            pltpu.VMEM((RANKS, TOK, LANES), BF16),
            pltpu.VMEM((2, TOK, 4096), BF16),
            pltpu.VMEM((256, 4096), BF16),
            pltpu.VMEM((2, LEN, QB), F32),
            pltpu.VMEM((LEN, LANES), F32),
            pltpu.VMEM(tile, F32),
            pltpu.VMEM((2, 8, LANES), F32),
            pltpu.VMEM(tile, F32),
            pltpu.VMEM(tile, F32),
            pltpu.VMEM((8, LANES), F32),
            pltpu.VMEM(tile, F32),
            pltpu.VMEM(tile, F32),
            pltpu.VMEM((8, LANES), F32),
            pltpu.VMEM(tile, F32),
            pltpu.VMEM((8, LANES), F32),
            pltpu.VMEM(tile, F32),
            pltpu.VMEM((HEADS, 8, LEN), F32),
            pltpu.VMEM((32, 256), F32),
            pltpu.VMEM((32, 256), F32),
            pltpu.VMEM((128, 256), F32),
            pltpu.SemaphoreType.DMA((N_SEM,)),
            pltpu.SemaphoreType.DMA((N_SEM,)),
        ],
        compiler_params=pltpu.CompilerParams(
            collective_id=0, has_side_effects=True, vmem_limit_bytes=48 * 2**20),
    )(q_proj, k_proj, v_proj, hidden_in, out_weight, doc_lengths, wide_pos)


def solution(mesh):
    return jax.shard_map(
        shards,
        mesh=mesh,
        in_specs=(
            P("dp", "seq", None),
            P("dp", "seq", None),
            P("dp", "seq", None),
            P("dp", "seq", None),
            P("seq", None),
            P("dp"),
            P(),
        ),
        out_specs=(P("dp"), P("seq", "dp")),
        check_vma=False,
    )
```

```python
import math

import jax
import jax.numpy as jnp
from jax import lax
from jax.experimental import pallas as pl
from jax.experimental.pallas import tpu as pltpu
from jax.sharding import PartitionSpec as P

MESH = pl.DeviceIdType.MESH
F32 = jnp.float32
BF16 = jnp.bfloat16
HIGHEST = lax.Precision.HIGHEST
LANES = 128
TOK = 128
RANKS = 16
HEADS = 4
LEN = 2048
QB = 256
EXP2_SCALE = math.log2(math.e) / math.sqrt(128.0)
INV_TEMP = 20.0
EPS = 1e-06

(K_SEM, Q_SEM, V_SEM, SIB_SEM, RS_SEM, RG_SEM, TG_SEM, PG_SEM, GRAM_SEM, HID_SEM, W_SEM,
 K_IN_SEM, Q_IN_SEM, V_IN_SEM, W_IN_SEM) = (0, 1, 5, 6, 7, 8, 9, 10, 11, 12, 13, 14, 15, 16, 17)
N_SEM = 18


def split3(x):
    hi = x.astype(BF16).astype(F32)
    mid = (x - hi).astype(BF16).astype(F32)
    lo = x - hi - mid
    return hi, mid, lo


def kernel(
    q_hbm, k_hbm, v_hbm, hid_ref, wt_ref, len_ref,
    end_ref,
    q_ref, k_ref, v_ref, qbuf, kbuf, vbuf, hbuf, wbuf, sbuf, wsum, resid,
    sib, rs_out, rs_buf, rtile, rg_buf, tg_buf, ptile, pg_buf, gtile, gram_buf,
    lhs_ref, rg_mat,
    send_sem, recv_sem, sync,
):
    g = lax.axis_index("dp")
    s = lax.axis_index("seq")
    core = s % 2
    col = (s // 2) % 4
    row = s // 8

    def seq_peer(e):
        odd = e % 2
        i = (e // 2) % 4
        dc = 1 - e // 8
        dx = (i + 3 - 2 * odd) % 4
        return ((row + 1 - odd) % 2) * 8 + ((col + dx) % 4) * 2 + (core + dc) % 2

    k_copy = pltpu.make_async_copy(k_hbm, k_ref, recv_sem.at[K_IN_SEM])
    k_copy.start()
    q_copy = pltpu.make_async_copy(q_hbm, q_ref, recv_sem.at[Q_IN_SEM])
    q_copy.start()
    v_copy = pltpu.make_async_copy(v_hbm, v_ref, recv_sem.at[V_IN_SEM])
    v_copy.start()
    hid_copy = pltpu.make_async_copy(hid_ref, hbuf, recv_sem.at[HID_SEM])
    hid_copy.start()
    wt_copy = pltpu.make_async_copy(wt_ref, wbuf.at[core], recv_sem.at[W_IN_SEM])
    wt_copy.start()

    z = g // 2
    y_hi = g % 2
    sibling = (g, s + 1 - 2 * core)
    z_next = (((z + 1) % 8) * 2 + y_hi, s)
    z_prev = (((z + 7) % 8) * 2 + y_hi, s)
    far_half = (z * 2 + 1 - y_hi, s)

    def signal(sem, *targets):
        for target in targets:
            pl.semaphore_signal(sem, inc=1, device_id=target, device_id_type=MESH)

    barrier = pltpu.get_barrier_semaphore()
    signal(barrier, far_half, z_next, z_prev)

    def greet(e, c):
        signal(barrier, (g, seq_peer(e)))
        return c

    lax.fori_loop(0, RANKS - 1, greet, 0)
    pl.semaphore_wait(barrier, RANKS + 2)

    def remote(src, dst, sem, target):
        pltpu.make_async_remote_copy(
            src_ref=src, dst_ref=dst, send_sem=send_sem.at[sem], recv_sem=recv_sem.at[sem],
            device_id=target, device_id_type=MESH,
        ).start()

    def cols(first):
        return pl.ds(pl.multiple_of(first * LANES, LANES), LANES)

    def send_k(e, c):
        t = seq_peer(e)
        remote(k_ref.at[t % 2, :, cols(t // 2)], kbuf.at[s], K_SEM, (g, t))
        return c

    def send_q(h):
        def body(e, c):
            t = seq_peer(e)
            remote(q_ref.at[t % 2, :, cols((t // 2) * HEADS + h)], qbuf.at[h, s], Q_SEM + h, (g, t))
            return c
        return body

    def send_v(e, c):
        t = seq_peer(e)
        remote(v_ref.at[t % 2, :, cols(t // 2)], vbuf.at[s], V_SEM, (g, t))
        return c

    k_copy.wait()
    pltpu.make_async_copy(k_ref.at[core, :, cols(s // 2)], kbuf.at[s], recv_sem.at[K_SEM]).start()
    lax.fori_loop(0, RANKS - 1, send_k, 0)

    q_copy.wait()
    v_copy.wait()

    def send_head(h, c):
        pltpu.make_async_copy(
            q_ref.at[core, :, cols((s // 2) * HEADS + h)], qbuf.at[h, s], recv_sem.at[Q_SEM + h]
        ).start()
        lax.fori_loop(0, RANKS - 1, send_q(h), 0)
        return c

    lax.fori_loop(0, HEADS, send_head, 0)
    pltpu.make_async_copy(v_ref.at[core, :, cols(s // 2)], vbuf.at[s], recv_sem.at[V_SEM]).start()
    lax.fori_loop(0, RANKS - 1, send_v, 0)

    wt_copy.wait()
    remote(wbuf.at[core], wbuf.at[core], W_SEM, sibling)

    for r in range(4):
        signal(sync.at[r], z_next, z_prev)
        pl.semaphore_wait(sync.at[r], 2)
    signal(sync.at[4], far_half)
    pl.semaphore_wait(sync.at[4], 1)

    def wait_all(ref, sem):
        pltpu.make_async_copy(ref, ref, sem).wait()

    len0 = len_ref[0]
    len1 = len_ref[1]

    hid_copy.wait()
    place = s * TOK + lax.broadcasted_iota(jnp.int32, (16, TOK), 1)
    ones = jnp.ones((16, TOK), F32)
    zeros = jnp.zeros((16, TOK), F32)
    for doc, length in ((0, len0), (1, len1)):
        mask = jnp.where(place < length, ones, zeros).astype(BF16)
        inv_len = jnp.full((1, 1), 1.0, F32) / jnp.full((1, 1), length, jnp.int32).astype(F32)

        def add_resid(t, c, doc=doc, mask=mask, inv_len=inv_len):
            part = jnp.dot(
                mask, hbuf[doc, :, pl.ds(pl.multiple_of(t * 256, 256), 256)],
                preferred_element_type=F32) * inv_len
            resid[t, doc:doc + 1, :] = part[0:1, 0:LANES]
            resid[t, 2 + doc:3 + doc, :] = part[0:1, LANES:]
            return c

        lax.fori_loop(0, RANKS, add_resid, 0)

    my_len = len_ref[core]

    wait_all(kbuf, recv_sem.at[K_SEM])

    def one_head(h, c):
        wait_all(qbuf.at[h], recv_sem.at[Q_SEM + h])
        for i in range(LEN // QB):
            n = (i + 1) * QB
            nb = n // TOK
            keys = kbuf[0:nb].reshape(n, LANES)
            queries = qbuf[h, 2 * i:2 * i + 2].reshape(QB, LANES)
            sref = sbuf.at[i % 2]
            sref[0:n, :] = lax.dot_general(
                keys, queries, (((1,), (1,)), ((), ())), preferred_element_type=F32)
            diag = sref[n - QB:n, :]
            vis = lax.broadcasted_iota(jnp.int32, (QB, QB), 0) <= lax.broadcasted_iota(
                jnp.int32, (QB, QB), 1)
            sref[n - QB:n, :] = jnp.where(vis, diag, -1e30)
            peak = sref[0:8, :]
            for r in range(8, n, 8):
                peak = jnp.maximum(peak, sref[r:r + 8, :])
            peak = jnp.max(peak, axis=0, keepdims=True)
            total = jnp.zeros((8, QB), F32)
            step = 64
            for r in range(0, n, step):
                e = jnp.exp2((sref[r:r + step, :] - peak) * EXP2_SCALE)
                sref[r:r + step, :] = e
                total = total + jnp.sum(e.reshape(step // 8, 8, QB), axis=0)
            total = jnp.sum(total, axis=0, keepdims=True)
            t_at = i * QB + lax.broadcasted_iota(jnp.int32, (1, QB), 1)
            ratio = jnp.where(t_at < my_len, 1.0 / total, 0.0)
            for r in range(0, n, step):
                e = sref[r:r + step, :] * ratio
                e = e[:, 0:LANES] + e[:, LANES:]
                if r >= n - QB:
                    wsum[r:r + step, :] = e
                else:
                    wsum[r:r + step, :] += e
        lane_ones = jnp.ones((8, LANES), F32)
        w_row = lax.dot_general(
            lane_ones, wsum[...], (((1,), (1,)), ((), ())), precision=HIGHEST,
            preferred_element_type=F32)
        for p, part in enumerate(split3(w_row[0:1])):
            lhs_ref[pl.ds(p * HEADS + h, 1), :] = part
        return c

    lhs_ref[12:16, :] = jnp.zeros((4, LEN), F32)
    lax.fori_loop(0, HEADS, one_head, 0)
    lhs = lhs_ref[...].astype(BF16)

    wait_all(vbuf, recv_sem.at[V_SEM])
    inv_my_len = jnp.full((1, 1), 1.0, F32) / jnp.full((1, 1), my_len, jnp.int32).astype(F32)
    out = jnp.dot(lhs, vbuf[...].reshape(LEN, LANES), preferred_element_type=F32)
    mine = (out[0:4] + out[4:8] + out[8:12]) * inv_my_len

    wide_mine = jnp.concatenate([mine[h:h + 1] for h in range(HEADS)], axis=1)
    lhs2 = jnp.concatenate(
        list(split3(wide_mine)) + [jnp.zeros((13, HEADS * LANES), F32)], axis=0).astype(BF16)
    wait_all(wbuf.at[0], recv_sem.at[W_SEM])
    part = jnp.dot(
        lhs2, wbuf[...].reshape(HEADS * LANES, 4096), preferred_element_type=F32)
    part = part[0:1] + part[1:2] + part[2:3]
    tile_row = lax.broadcasted_iota(jnp.int32, (4, LANES), 0)
    for t in range(RANKS):
        rs_out[t] = resid[t] + jnp.where(
            tile_row == core, part[:, 256 * t:256 * t + LANES],
            jnp.where(tile_row == 2 + core, part[:, 256 * t + LANES:256 * t + 256], 0.0))

    def send_partial(e, c):
        t = seq_peer(e)
        remote(rs_out.at[t], rs_buf.at[y_hi * RANKS + s], RS_SEM, (g, t))
        remote(rs_out.at[t], rs_buf.at[y_hi * RANKS + s], RS_SEM, (z * 2 + 1 - y_hi, t))
        return c

    lax.fori_loop(0, RANKS - 1, send_partial, 0)
    remote(rs_out.at[s], rs_buf.at[y_hi * RANKS + s], RS_SEM, far_half)
    rs_buf[y_hi * RANKS + s] = rs_out[s]

    sib[core] = mine
    remote(sib.at[core], sib.at[core], SIB_SEM, sibling)
    wait_all(sib.at[0], recv_sem.at[SIB_SEM])
    low = core == 0
    doc0 = jnp.where(low, sib[0, 0:2, :], sib[0, 2:4, :])
    doc1 = jnp.where(low, sib[1, 0:2, :], sib[1, 2:4, :])
    both = jnp.concatenate([doc0[0:1], doc1[0:1], doc0[1:2], doc1[1:2]], axis=0)
    ptile[...] = both
    pg_buf[g] = both

    def send_pooled(e, c):
        remote(ptile, pg_buf.at[g], PG_SEM, ((g + e + 1) % RANKS, s))
        return c

    lax.fori_loop(0, RANKS - 1, send_pooled, 0)

    wait_all(rs_buf.at[pl.ds(0, 2 * RANKS - 1)], recv_sem.at[RS_SEM])
    for half in range(2):
        raw = jnp.sum(rs_buf[half * RANKS:(half + 1) * RANKS], axis=0)
        rtile[half] = raw
        rg_buf[z, half] = raw

    def send_raw(e, c):
        remote(rtile, rg_buf.at[z], RG_SEM, (((z + e + 1) % 8) * 2 + y_hi, s))
        return c

    lax.fori_loop(0, 7, send_raw, 0)

    @pl.when(s == g)
    def _():
        tg_buf[g] = rtile[y_hi]

    def send_cols(e, c):
        @pl.when(jnp.logical_or(s != g, e != s))
        def _():
            remote(rtile.at[y_hi], tg_buf.at[g], TG_SEM, (s, e))
        return c

    lax.fori_loop(0, RANKS, send_cols, 0)

    wait_all(rg_buf.at[pl.ds(0, 7)], recv_sem.at[RG_SEM])
    for d in range(RANKS):
        for half in range(2):
            piece = rg_buf[d // 2, d % 2, 2 * half:2 * half + 2, :]
            for rep in range(4):
                rg_mat[32 * rep + 2 * d:32 * rep + 2 * d + 2, half * LANES:(half + 1) * LANES] = piece
    wide = lax.dot_general(
        rg_mat[0:32, :], rg_mat[...], (((1,), (1,)), ((), ())), precision=HIGHEST,
        preferred_element_type=F32)
    lane_group = lax.broadcasted_iota(jnp.int32, (8, LANES), 1) // 32
    packed = jnp.zeros((8, LANES), F32)
    for p in range(4):
        packed = packed + jnp.where(lane_group == p, wide[8 * p:8 * p + 8], 0.0)
    gtile[...] = packed
    gram_buf[s] = packed

    def send_gram(e, c):
        remote(gtile, gram_buf.at[s], GRAM_SEM, (g, seq_peer(e)))
        return c

    lax.fori_loop(0, RANKS - 1, send_gram, 0)

    wait_all(pg_buf.at[pl.ds(0, RANKS - 1)], recv_sem.at[PG_SEM])
    for d in range(RANKS):
        for half in range(2):
            end_ref[2 * d:2 * d + 2, half * LANES:(half + 1) * LANES] = pg_buf[
                d, 2 * half:2 * half + 2, :]

    @pl.when(s == g)
    def _():
        wait_all(tg_buf.at[pl.ds(0, RANKS - 1)], recv_sem.at[TG_SEM])

    @pl.when(s != g)
    def _():
        wait_all(tg_buf, recv_sem.at[TG_SEM])

    for d in range(RANKS):
        for half in range(2):
            end_ref[32 + 2 * d:34 + 2 * d, half * LANES:(half + 1) * LANES] = tg_buf[
                d, 2 * half:2 * half + 2, :]

    wait_all(gram_buf.at[pl.ds(0, RANKS - 1)], recv_sem.at[GRAM_SEM])
    gp = jnp.sum(gram_buf[...], axis=0)
    end_ref[64:72, 0:LANES] = gp
    end_ref[64:72, LANES:] = gp

    some = RANKS - 1
    wait_all(kbuf.at[pl.ds(0, some)], send_sem.at[K_SEM])
    for h in range(HEADS):
        wait_all(qbuf.at[h, pl.ds(0, some)], send_sem.at[Q_SEM + h])
    wait_all(vbuf.at[pl.ds(0, some)], send_sem.at[V_SEM])
    wait_all(sib.at[0], send_sem.at[SIB_SEM])
    wait_all(wbuf.at[0], send_sem.at[W_SEM])
    wait_all(rs_buf.at[pl.ds(0, 2 * RANKS - 1)], send_sem.at[RS_SEM])
    wait_all(rg_buf.at[pl.ds(0, 7)], send_sem.at[RG_SEM])

    @pl.when(s == g)
    def _():
        wait_all(tg_buf.at[pl.ds(0, some)], send_sem.at[TG_SEM])

    @pl.when(s != g)
    def _():
        wait_all(tg_buf, send_sem.at[TG_SEM])

    wait_all(pg_buf.at[pl.ds(0, some)], send_sem.at[PG_SEM])
    wait_all(gram_buf.at[pl.ds(0, some)], send_sem.at[GRAM_SEM])


def finish(end_ref, pos_ref, cost_ref, wo_ref):
    g = lax.axis_index("dp")
    pooled = end_ref[0:32, :]
    raw = end_ref[32:64, :]
    gp = end_ref[64:72, 0:LANES]
    ri = lax.broadcasted_iota(jnp.int32, (32, 32), 0)
    ci = lax.broadcasted_iota(jnp.int32, (32, 32), 1)
    eye = ri == ci
    eye_f = jnp.where(eye, 1.0, 0.0)
    hot_t = jnp.where(ri == pos_ref[...], 1.0, 0.0)
    hot = lax.dot_general(
        eye_f, hot_t, (((1,), (1,)), ((), ())), precision=HIGHEST, preferred_element_type=F32)
    gram = jnp.concatenate(
        [gp if p == 0 else pltpu.roll(gp, LANES - 32 * p, 1) for p in range(4)], axis=0)[:, 0:32]
    on_diag = jnp.where(eye, gram, 0.0)
    sq_i = jnp.sum(on_diag, axis=1, keepdims=True) + EPS
    sq_j = jnp.sum(on_diag, axis=0, keepdims=True) + EPS
    inv_i = lax.rsqrt(sq_i)
    inv_j = lax.rsqrt(sq_j)
    sims = gram * inv_i * inv_j * INV_TEMP
    raised = jnp.where(eye, 0.0, jnp.exp(sims - INV_TEMP))
    tot_i = jnp.sum(raised, axis=1, keepdims=True)
    tot_j = jnp.sum(raised, axis=0, keepdims=True)
    cost = jnp.log(tot_i) + INV_TEMP - jnp.sum(sims * hot, axis=1, keepdims=True)
    both_grad = raised / tot_i + raised / tot_j - hot - hot_t
    weighted = both_grad * inv_j * INV_TEMP
    along = jnp.sum(weighted * gram, axis=1, keepdims=True)
    coef = inv_i * weighted - eye_f * (inv_i * along / sq_i)
    grad_raw = jnp.dot(coef, raw, precision=HIGHEST, preferred_element_type=F32)
    wo_ref[...] = lax.dot_general(
        pooled, grad_raw, (((0,), (0,)), ((), ())), precision=HIGHEST,
        preferred_element_type=F32)
    doc_at = lax.broadcasted_iota(jnp.int32, (32, 1), 0)
    cost_ref[0] = jnp.sum(jnp.where(doc_at == 2 * g, cost, 0.0))
    cost_ref[1] = jnp.sum(jnp.where(doc_at == 2 * g + 1, cost, 0.0))


def shards(q_proj, k_proj, v_proj, hidden_in, out_weight, doc_lengths, positive):
    any_spec = pl.BlockSpec(memory_space=pltpu.HBM)
    smem = pl.BlockSpec(memory_space=pltpu.SMEM)
    vmem = pl.BlockSpec(memory_space=pltpu.VMEM)
    tile = (RANKS, 4, LANES)
    end = pl.pallas_call(
        kernel,
        out_shape=jax.ShapeDtypeStruct((72, 256), F32),
        in_specs=[any_spec] * 5 + [smem],
        out_specs=vmem,
        scratch_shapes=[
            pltpu.VMEM((2, TOK, 4096), BF16),
            pltpu.VMEM((2, TOK, 1024), BF16),
            pltpu.VMEM((2, TOK, 1024), BF16),
            pltpu.VMEM((HEADS, RANKS, TOK, LANES), BF16),
            pltpu.VMEM((RANKS, TOK, LANES), BF16),
            pltpu.VMEM((RANKS, TOK, LANES), BF16),
            pltpu.VMEM((2, TOK, 4096), BF16),
            pltpu.VMEM((2, 256, 4096), BF16),
            pltpu.VMEM((2, LEN, QB), F32),
            pltpu.VMEM((LEN, LANES), F32),
            pltpu.VMEM(tile, F32),
            pltpu.VMEM((2, 4, LANES), F32),
            pltpu.VMEM(tile, F32),
            pltpu.VMEM((2 * RANKS, 4, LANES), F32),
            pltpu.VMEM((2, 4, LANES), F32),
            pltpu.VMEM((8, 2, 4, LANES), F32),
            pltpu.VMEM(tile, F32),
            pltpu.VMEM((4, LANES), F32),
            pltpu.VMEM(tile, F32),
            pltpu.VMEM((8, LANES), F32),
            pltpu.VMEM((RANKS, 8, LANES), F32),
            pltpu.VMEM((16, LEN), F32),
            pltpu.VMEM((128, 256), F32),
            pltpu.SemaphoreType.DMA((N_SEM,)),
            pltpu.SemaphoreType.DMA((N_SEM,)),
            pltpu.SemaphoreType.REGULAR((5,)),
        ],
        compiler_params=pltpu.CompilerParams(
            collective_id=0, has_side_effects=True, vmem_limit_bytes=60 * 2**20),
    )(q_proj, k_proj, v_proj, hidden_in, out_weight, doc_lengths)
    return pl.pallas_call(
        finish,
        out_shape=(
            jax.ShapeDtypeStruct((2,), F32),
            jax.ShapeDtypeStruct((256, 256), F32),
        ),
        in_specs=[vmem] * 2,
        out_specs=(smem, vmem),
        compiler_params=pltpu.CompilerParams(vmem_limit_bytes=60 * 2**20),
    )(end, positive.reshape(1, 32))


def solution(mesh):
    return jax.shard_map(
        shards,
        mesh=mesh,
        in_specs=(
            P("dp", "seq", None),
            P("dp", "seq", None),
            P("dp", "seq", None),
            P("dp", "seq", None),
            P("seq", None),
            P("dp"),
            P(),
        ),
        out_specs=(P("dp"), P("seq", "dp")),
        check_vma=False,
    )
```

```python
import math

import jax
import jax.numpy as jnp
from jax import lax
from jax.experimental import pallas as pl
from jax.experimental.pallas import tpu as pltpu
from jax.sharding import PartitionSpec as P

MESH = pl.DeviceIdType.MESH
F32 = jnp.float32
BF16 = jnp.bfloat16
HIGHEST = lax.Precision.HIGHEST
LANES = 128
TOK = 128
RANKS = 16
HEADS = 4
LEN = 2048
QB = 256
EXP2_SCALE = math.log2(math.e) / math.sqrt(128.0)
INV_TEMP = 20.0
EPS = 1e-06

(K_SEM, Q_SEM, V_SEM, SIB_SEM, RS_SEM, RG_SEM, TG_SEM, PG_SEM, GRAM_SEM, HID_SEM, W_SEM,
 K_IN_SEM, Q_IN_SEM, V_IN_SEM, W_IN_SEM) = (0, 1, 5, 6, 7, 8, 9, 10, 11, 12, 13, 14, 15, 16, 17)
N_SEM = 18


def split3(x):
    hi = x.astype(BF16).astype(F32)
    mid = (x - hi).astype(BF16).astype(F32)
    lo = x - hi - mid
    return hi, mid, lo


def kernel(
    q_hbm, k_hbm, v_hbm, hid_ref, wt_ref, len_ref,
    end_ref,
    q_ref, k_ref, v_ref, qbuf, kbuf, vbuf, hbuf, wbuf, sbuf, wsum, resid,
    sib, rs_out, rs_buf, rtile, rg_buf, tg_buf, ptile, pg_buf, gtile, gram_buf,
    lhs_ref, rg_mat,
    send_sem, recv_sem, sync,
):
    g = lax.axis_index("dp")
    s = lax.axis_index("seq")
    core = s % 2
    col = (s // 2) % 4
    row = s // 8

    rows = [row * 8, (1 - row) * 8]
    ring = [((col + dx) % 4) * 2 for dx in range(4)]
    cores = [core, 1 - core]

    def at(dy, dx, dc):
        return rows[dy] + ring[dx] + cores[dc]

    peers = []
    for dc in range(2):
        for dx in (2, 1, 0, 3):
            peers.append(at(1, dx, dc))
            if dc or dx != 2:
                peers.append(at(0, (dx + 2) % 4, dc))

    k_copy = pltpu.make_async_copy(k_hbm, k_ref, recv_sem.at[K_IN_SEM])
    k_copy.start()
    q_copy = pltpu.make_async_copy(q_hbm, q_ref, recv_sem.at[Q_IN_SEM])
    q_copy.start()
    v_copy = pltpu.make_async_copy(v_hbm, v_ref, recv_sem.at[V_IN_SEM])
    v_copy.start()
    hid_copy = pltpu.make_async_copy(hid_ref, hbuf, recv_sem.at[HID_SEM])
    hid_copy.start()
    wt_copy = pltpu.make_async_copy(wt_ref, wbuf.at[core], recv_sem.at[W_IN_SEM])
    wt_copy.start()

    z = g // 2
    y_hi = g % 2
    sibling = (g, s + 1 - 2 * core)
    z_next = (((z + 1) % 8) * 2 + y_hi, s)
    z_prev = (((z + 7) % 8) * 2 + y_hi, s)
    far_half = (z * 2 + 1 - y_hi, s)

    def signal(sem, *targets):
        for target in targets:
            pl.semaphore_signal(sem, inc=1, device_id=target, device_id_type=MESH)

    barrier = pltpu.get_barrier_semaphore()
    signal(barrier, far_half, z_next, z_prev)

    for t in peers:
        signal(barrier, (g, t))
    pl.semaphore_wait(barrier, RANKS + 2)

    def remote(src, dst, sem, target):
        pltpu.make_async_remote_copy(
            src_ref=src, dst_ref=dst, send_sem=send_sem.at[sem], recv_sem=recv_sem.at[sem],
            device_id=target, device_id_type=MESH,
        ).start()

    def cols(first):
        return pl.ds(pl.multiple_of(first * LANES, LANES), LANES)

    k_copy.wait()
    pltpu.make_async_copy(k_ref.at[core, :, cols(s // 2)], kbuf.at[s], recv_sem.at[K_SEM]).start()
    for t in peers:
        remote(k_ref.at[t % 2, :, cols(t // 2)], kbuf.at[s], K_SEM, (g, t))

    q_copy.wait()
    v_copy.wait()

    def send_head(h, c):
        pltpu.make_async_copy(
            q_ref.at[core, :, cols((s // 2) * HEADS + h)], qbuf.at[h, s], recv_sem.at[Q_SEM + h]
        ).start()
        for t in peers:
            remote(q_ref.at[t % 2, :, cols((t // 2) * HEADS + h)], qbuf.at[h, s], Q_SEM + h, (g, t))
        return c

    lax.fori_loop(0, HEADS, send_head, 0)
    pltpu.make_async_copy(v_ref.at[core, :, cols(s // 2)], vbuf.at[s], recv_sem.at[V_SEM]).start()
    for t in peers:
        remote(v_ref.at[t % 2, :, cols(t // 2)], vbuf.at[s], V_SEM, (g, t))

    wt_copy.wait()
    remote(wbuf.at[core], wbuf.at[core], W_SEM, sibling)

    def wait_all(ref, sem):
        pltpu.make_async_copy(ref, ref, sem).wait()

    len0 = len_ref[0]
    len1 = len_ref[1]

    hid_copy.wait()
    place = s * TOK + lax.broadcasted_iota(jnp.int32, (16, TOK), 1)
    ones = jnp.ones((16, TOK), F32)
    zeros = jnp.zeros((16, TOK), F32)
    for doc, length in ((0, len0), (1, len1)):
        mask = jnp.where(place < length, ones, zeros).astype(BF16)
        inv_len = jnp.full((1, 1), 1.0, F32) / jnp.full((1, 1), length, jnp.int32).astype(F32)

        part = jnp.dot(mask, hbuf[doc], preferred_element_type=F32)[0:1] * inv_len
        for t in range(RANKS):
            resid[t, doc:doc + 1, :] = part[:, 256 * t:256 * t + LANES]
            resid[t, 2 + doc:3 + doc, :] = part[:, 256 * t + LANES:256 * t + 256]

    my_len = len_ref[core]

    wait_all(kbuf, recv_sem.at[K_SEM])

    def one_head(h, c):
        signal(sync.at[h], z_next, z_prev)
        wait_all(qbuf.at[h], recv_sem.at[Q_SEM + h])
        for i in range(LEN // QB):
            n = (i + 1) * QB
            nb = n // TOK
            keys = kbuf[0:nb].reshape(n, LANES)
            queries = qbuf[h, 2 * i:2 * i + 2].reshape(QB, LANES)
            sref = sbuf.at[i % 2]
            sref[0:n, :] = lax.dot_general(
                keys, queries, (((1,), (1,)), ((), ())), preferred_element_type=F32)
            diag = sref[n - QB:n, :]
            vis = lax.broadcasted_iota(jnp.int32, (QB, QB), 0) <= lax.broadcasted_iota(
                jnp.int32, (QB, QB), 1)
            sref[n - QB:n, :] = jnp.where(vis, diag, -1e30)
            peak = sref[0:8, :]
            for r in range(8, n, 8):
                peak = jnp.maximum(peak, sref[r:r + 8, :])
            peak = jnp.max(peak, axis=0, keepdims=True)
            total = jnp.zeros((8, QB), F32)
            step = 64
            for r in range(0, n, step):
                e = jnp.exp2((sref[r:r + step, :] - peak) * EXP2_SCALE)
                sref[r:r + step, :] = e
                total = total + jnp.sum(e.reshape(step // 8, 8, QB), axis=0)
            total = jnp.sum(total, axis=0, keepdims=True)
            t_at = i * QB + lax.broadcasted_iota(jnp.int32, (1, QB), 1)
            ratio = jnp.where(t_at < my_len, 1.0 / total, 0.0)
            for r in range(0, n, step):
                e = sref[r:r + step, :] * ratio
                e = e[:, 0:LANES] + e[:, LANES:]
                if r >= n - QB:
                    wsum[r:r + step, :] = e
                else:
                    wsum[r:r + step, :] += e
        lane_ones = jnp.ones((8, LANES), F32)
        w_row = lax.dot_general(
            lane_ones, wsum[...], (((1,), (1,)), ((), ())), precision=HIGHEST,
            preferred_element_type=F32)
        for p, part in enumerate(split3(w_row[0:1])):
            lhs_ref[pl.ds(p * HEADS + h, 1), :] = part
        pl.semaphore_wait(sync.at[h], 2)
        return c

    lhs_ref[12:16, :] = jnp.zeros((4, LEN), F32)
    lax.fori_loop(0, HEADS, one_head, 0)
    signal(sync.at[HEADS], far_half)
    lhs = lhs_ref[...].astype(BF16)

    wait_all(vbuf, recv_sem.at[V_SEM])
    inv_my_len = jnp.full((1, 1), 1.0, F32) / jnp.full((1, 1), my_len, jnp.int32).astype(F32)
    out = jnp.dot(lhs, vbuf[...].reshape(LEN, LANES), preferred_element_type=F32)
    mine = (out[0:4] + out[4:8] + out[8:12]) * inv_my_len

    pl.semaphore_wait(sync.at[HEADS], 1)

    wide_mine = jnp.concatenate([mine[h:h + 1] for h in range(HEADS)], axis=1)
    lhs2 = jnp.concatenate(
        list(split3(wide_mine)) + [jnp.zeros((13, HEADS * LANES), F32)], axis=0).astype(BF16)
    wait_all(wbuf.at[0], recv_sem.at[W_SEM])
    tile_row = lax.broadcasted_iota(jnp.int32, (4, LANES), 0)

    for dy in (1, 0):
        part = jnp.dot(
            lhs2,
            wbuf[:, :, pl.ds(pl.multiple_of(rows[dy] * 256, 2048), 2048)].reshape(
                HEADS * LANES, 2048),
            preferred_element_type=F32)
        part = part[0:1] + part[1:2] + part[2:3]
        for k in range(8):
            rs_out[rows[dy] + k] = resid[rows[dy] + k] + jnp.where(
                tile_row == core, part[:, 256 * k:256 * k + LANES],
                jnp.where(tile_row == 2 + core, part[:, 256 * k + LANES:256 * k + 256], 0.0))
        for dx in (2, 1, 3, 0):
            for dc in (1, 0):
                t = at(dy, dx, dc)
                mine_there = rs_buf.at[y_hi * RANKS + s]
                remote(rs_out.at[t], mine_there, RS_SEM, (z * 2 + 1 - y_hi, t))
                if dy or dx or dc:
                    remote(rs_out.at[t], mine_there, RS_SEM, (g, t))
    rs_buf[y_hi * RANKS + s] = rs_out[s]

    sib[core] = mine
    remote(sib.at[core], sib.at[core], SIB_SEM, sibling)
    wait_all(sib.at[0], recv_sem.at[SIB_SEM])
    low = core == 0
    doc0 = jnp.where(low, sib[0, 0:2, :], sib[0, 2:4, :])
    doc1 = jnp.where(low, sib[1, 0:2, :], sib[1, 2:4, :])
    both = jnp.concatenate([doc0[0:1], doc1[0:1], doc0[1:2], doc1[1:2]], axis=0)
    ptile[...] = both
    pg_buf[g] = both

    def send_pooled(e, c):
        remote(ptile, pg_buf.at[g], PG_SEM, (lax.rem(g + e + 1, RANKS), s))
        return c

    lax.fori_loop(0, RANKS - 1, send_pooled, 0)

    wait_all(rs_buf.at[pl.ds(0, 2 * RANKS - 1)], recv_sem.at[RS_SEM])
    for half in range(2):
        raw = jnp.sum(rs_buf[half * RANKS:(half + 1) * RANKS], axis=0)
        rtile[half] = raw
        rg_buf[z, half] = raw

    for dz in (4, 3, 5, 2, 6, 1, 7):
        remote(rtile, rg_buf.at[z], RG_SEM, (((z + dz) % 8) * 2 + y_hi, s))

    @pl.when(s == g)
    def _():
        tg_buf[g] = rtile[y_hi]

    def send_cols(e, c):
        @pl.when(jnp.logical_or(s != g, e != s))
        def _():
            remote(rtile.at[y_hi], tg_buf.at[g], TG_SEM, (s, e))
        return c

    lax.fori_loop(0, RANKS, send_cols, 0)

    wait_all(rg_buf.at[pl.ds(0, 7)], recv_sem.at[RG_SEM])
    for d in range(RANKS):
        for half in range(2):
            piece = rg_buf[d // 2, d % 2, 2 * half:2 * half + 2, :]
            for rep in range(4):
                rg_mat[32 * rep + 2 * d:32 * rep + 2 * d + 2, half * LANES:(half + 1) * LANES] = piece
    wide = lax.dot_general(
        rg_mat[0:32, :], rg_mat[...], (((1,), (1,)), ((), ())), precision=HIGHEST,
        preferred_element_type=F32)
    lane_group = lax.broadcasted_iota(jnp.int32, (8, LANES), 1) // 32
    packed = jnp.zeros((8, LANES), F32)
    for p in range(4):
        packed = packed + jnp.where(lane_group == p, wide[8 * p:8 * p + 8], 0.0)
    gtile[...] = packed
    gram_buf[s] = packed

    for t in peers:
        remote(gtile, gram_buf.at[s], GRAM_SEM, (g, t))

    wait_all(pg_buf.at[pl.ds(0, RANKS - 1)], recv_sem.at[PG_SEM])
    for d in range(RANKS):
        for half in range(2):
            end_ref[2 * d:2 * d + 2, half * LANES:(half + 1) * LANES] = pg_buf[
                d, 2 * half:2 * half + 2, :]

    @pl.when(s == g)
    def _():
        wait_all(tg_buf.at[pl.ds(0, RANKS - 1)], recv_sem.at[TG_SEM])

    @pl.when(s != g)
    def _():
        wait_all(tg_buf, recv_sem.at[TG_SEM])

    for d in range(RANKS):
        for half in range(2):
            end_ref[32 + 2 * d:34 + 2 * d, half * LANES:(half + 1) * LANES] = tg_buf[
                d, 2 * half:2 * half + 2, :]

    wait_all(gram_buf.at[pl.ds(0, RANKS - 1)], recv_sem.at[GRAM_SEM])
    gp = jnp.sum(gram_buf[...], axis=0)
    end_ref[64:72, 0:LANES] = gp
    end_ref[64:72, LANES:] = gp

    some = RANKS - 1
    wait_all(kbuf.at[pl.ds(0, some)], send_sem.at[K_SEM])
    for h in range(HEADS):
        wait_all(qbuf.at[h, pl.ds(0, some)], send_sem.at[Q_SEM + h])
    wait_all(vbuf.at[pl.ds(0, some)], send_sem.at[V_SEM])
    wait_all(sib.at[0], send_sem.at[SIB_SEM])
    wait_all(wbuf.at[0], send_sem.at[W_SEM])
    wait_all(rs_buf.at[pl.ds(0, 2 * RANKS - 1)], send_sem.at[RS_SEM])
    wait_all(rg_buf.at[pl.ds(0, 7)], send_sem.at[RG_SEM])

    @pl.when(s == g)
    def _():
        wait_all(tg_buf.at[pl.ds(0, some)], send_sem.at[TG_SEM])

    @pl.when(s != g)
    def _():
        wait_all(tg_buf, send_sem.at[TG_SEM])

    wait_all(pg_buf.at[pl.ds(0, some)], send_sem.at[PG_SEM])
    wait_all(gram_buf.at[pl.ds(0, some)], send_sem.at[GRAM_SEM])


def finish(end_ref, pos_ref, cost_ref, wo_ref):
    g = lax.axis_index("dp")
    pooled = end_ref[0:32, :]
    raw = end_ref[32:64, :]
    gp = end_ref[64:72, 0:LANES]
    ri = lax.broadcasted_iota(jnp.int32, (32, 32), 0)
    ci = lax.broadcasted_iota(jnp.int32, (32, 32), 1)
    eye = ri == ci
    eye_f = jnp.where(eye, 1.0, 0.0)
    hot_t = jnp.where(ri == pos_ref[...], 1.0, 0.0)
    hot = lax.dot_general(
        eye_f, hot_t, (((1,), (1,)), ((), ())), precision=HIGHEST, preferred_element_type=F32)
    gram = jnp.concatenate(
        [gp if p == 0 else pltpu.roll(gp, LANES - 32 * p, 1) for p in range(4)], axis=0)[:, 0:32]
    on_diag = jnp.where(eye, gram, 0.0)
    sq_i = jnp.sum(on_diag, axis=1, keepdims=True) + EPS
    sq_j = jnp.sum(on_diag, axis=0, keepdims=True) + EPS
    inv_i = lax.rsqrt(sq_i)
    inv_j = lax.rsqrt(sq_j)
    sims = gram * inv_i * inv_j * INV_TEMP
    raised = jnp.where(eye, 0.0, jnp.exp(sims - INV_TEMP))
    tot_i = jnp.sum(raised, axis=1, keepdims=True)
    tot_j = jnp.sum(raised, axis=0, keepdims=True)
    cost = jnp.log(tot_i) + INV_TEMP - jnp.sum(sims * hot, axis=1, keepdims=True)
    both_grad = raised / tot_i + raised / tot_j - hot - hot_t
    weighted = both_grad * inv_j * INV_TEMP
    along = jnp.sum(weighted * gram, axis=1, keepdims=True)
    coef = inv_i * weighted - eye_f * (inv_i * along / sq_i)
    grad_raw = jnp.dot(coef, raw, precision=HIGHEST, preferred_element_type=F32)
    wo_ref[...] = lax.dot_general(
        pooled, grad_raw, (((0,), (0,)), ((), ())), precision=HIGHEST,
        preferred_element_type=F32)
    doc_at = lax.broadcasted_iota(jnp.int32, (32, 1), 0)
    cost_ref[0] = jnp.sum(jnp.where(doc_at == 2 * g, cost, 0.0))
    cost_ref[1] = jnp.sum(jnp.where(doc_at == 2 * g + 1, cost, 0.0))


def shards(q_proj, k_proj, v_proj, hidden_in, out_weight, doc_lengths, positive):
    any_spec = pl.BlockSpec(memory_space=pltpu.HBM)
    smem = pl.BlockSpec(memory_space=pltpu.SMEM)
    vmem = pl.BlockSpec(memory_space=pltpu.VMEM)
    tile = (RANKS, 4, LANES)
    end = pl.pallas_call(
        kernel,
        out_shape=jax.ShapeDtypeStruct((72, 256), F32),
        in_specs=[any_spec] * 5 + [smem],
        out_specs=vmem,
        scratch_shapes=[
            pltpu.VMEM((2, TOK, 4096), BF16),
            pltpu.VMEM((2, TOK, 1024), BF16),
            pltpu.VMEM((2, TOK, 1024), BF16),
            pltpu.VMEM((HEADS, RANKS, TOK, LANES), BF16),
            pltpu.VMEM((RANKS, TOK, LANES), BF16),
            pltpu.VMEM((RANKS, TOK, LANES), BF16),
            pltpu.VMEM((2, TOK, 4096), BF16),
            pltpu.VMEM((2, 256, 4096), BF16),
            pltpu.VMEM((2, LEN, QB), F32),
            pltpu.VMEM((LEN, LANES), F32),
            pltpu.VMEM(tile, F32),
            pltpu.VMEM((2, 4, LANES), F32),
            pltpu.VMEM(tile, F32),
            pltpu.VMEM((2 * RANKS, 4, LANES), F32),
            pltpu.VMEM((2, 4, LANES), F32),
            pltpu.VMEM((8, 2, 4, LANES), F32),
            pltpu.VMEM(tile, F32),
            pltpu.VMEM((4, LANES), F32),
            pltpu.VMEM(tile, F32),
            pltpu.VMEM((8, LANES), F32),
            pltpu.VMEM((RANKS, 8, LANES), F32),
            pltpu.VMEM((16, LEN), F32),
            pltpu.VMEM((128, 256), F32),
            pltpu.SemaphoreType.DMA((N_SEM,)),
            pltpu.SemaphoreType.DMA((N_SEM,)),
            pltpu.SemaphoreType.REGULAR((5,)),
        ],
        compiler_params=pltpu.CompilerParams(
            collective_id=0, has_side_effects=True, vmem_limit_bytes=107 * 2**19),
    )(q_proj, k_proj, v_proj, hidden_in, out_weight, doc_lengths)
    return pl.pallas_call(
        finish,
        out_shape=(
            jax.ShapeDtypeStruct((2,), F32),
            jax.ShapeDtypeStruct((256, 256), F32),
        ),
        in_specs=[vmem] * 2,
        out_specs=(smem, vmem),
        compiler_params=pltpu.CompilerParams(vmem_limit_bytes=107 * 2**19),
    )(end, positive.reshape(1, 32))


def solution(mesh):
    return jax.shard_map(
        shards,
        mesh=mesh,
        in_specs=(
            P("dp", "seq", None),
            P("dp", "seq", None),
            P("dp", "seq", None),
            P("dp", "seq", None),
            P("seq", None),
            P("dp"),
            P(),
        ),
        out_specs=(P("dp"), P("seq", "dp")),
        check_vma=False,
    )
```

```python
import math

import jax
import jax.numpy as jnp
from jax import lax
from jax.experimental import pallas as pl
from jax.experimental.pallas import tpu as pltpu
from jax.sharding import PartitionSpec as P

MESH = pl.DeviceIdType.MESH
F32 = jnp.float32
BF16 = jnp.bfloat16
HIGHEST = lax.Precision.HIGHEST
LANES = 128
TOK = 128
RANKS = 16
HEADS = 4
LEN = 2048
QB = 256
EXP2_SCALE = math.log2(math.e) / math.sqrt(128.0)
INV_TEMP = 20.0
EPS = 1e-06

(K_SEM, Q_SEM, V_SEM, SIB_SEM, RS_SEM, RG_SEM, TG_SEM, PG_SEM, GRAM_SEM, HID_SEM, W_SEM,
 K_IN_SEM, Q_IN_SEM, V_IN_SEM, W_IN_SEM) = (0, 1, 5, 6, 7, 8, 9, 10, 11, 12, 13, 14, 15, 16, 17)
N_SEM = 18


def split3(x):
    hi = x.astype(BF16).astype(F32)
    mid = (x - hi).astype(BF16).astype(F32)
    lo = x - hi - mid
    return hi, mid, lo


def kernel(
    q_hbm, k_hbm, v_hbm, hid_ref, wt_ref, len_ref,
    end_ref,
    q_ref, k_ref, v_ref, qbuf, kbuf, vbuf, hbuf, wbuf, sbuf, wsum, resid,
    sib, rs_out, rs_buf, rtile, rg_buf, tg_buf, ptile, pg_buf, gtile, gram_buf,
    lhs_ref, rg_mat,
    send_sem, recv_sem, sync,
):
    g = lax.axis_index("dp")
    s = lax.axis_index("seq")
    core = s % 2
    col = (s // 2) % 4
    row = s // 8

    rows = [row * 8, (1 - row) * 8]
    ring = [((col + dx) % 4) * 2 for dx in range(4)]
    cores = [core, 1 - core]

    def at(dy, dx, dc):
        return rows[dy] + ring[dx] + cores[dc]

    peers = []
    for dc in range(2):
        for dx in (2, 1, 0, 3):
            peers.append(at(1, dx, dc))
            if dc or dx != 2:
                peers.append(at(0, (dx + 2) % 4, dc))

    z = g // 2
    y_hi = g % 2
    sibling = (g, s + 1 - 2 * core)
    z_next = (((z + 1) % 8) * 2 + y_hi, s)
    z_prev = (((z + 7) % 8) * 2 + y_hi, s)
    far_half = (z * 2 + 1 - y_hi, s)

    def signal(sem, *targets):
        for target in targets:
            pl.semaphore_signal(sem, inc=1, device_id=target, device_id_type=MESH)

    barrier = pltpu.get_barrier_semaphore()
    for t in peers:
        signal(barrier, (g, t))
    signal(barrier, far_half, z_next, z_prev)

    k_copy = pltpu.make_async_copy(k_hbm, k_ref, recv_sem.at[K_IN_SEM])
    k_copy.start()
    q_copy = pltpu.make_async_copy(q_hbm, q_ref, recv_sem.at[Q_IN_SEM])
    q_copy.start()
    v_copy = pltpu.make_async_copy(v_hbm, v_ref, recv_sem.at[V_IN_SEM])
    v_copy.start()
    hid_copy = pltpu.make_async_copy(hid_ref, hbuf, recv_sem.at[HID_SEM])
    hid_copy.start()
    wt_copy = pltpu.make_async_copy(wt_ref, wbuf.at[core], recv_sem.at[W_IN_SEM])
    wt_copy.start()

    pl.semaphore_wait(barrier, RANKS + 2)

    def remote(src, dst, sem, target):
        pltpu.make_async_remote_copy(
            src_ref=src, dst_ref=dst, send_sem=send_sem.at[sem], recv_sem=recv_sem.at[sem],
            device_id=target, device_id_type=MESH,
        ).start()

    def cols(first):
        return pl.ds(pl.multiple_of(first * LANES, LANES), LANES)

    k_copy.wait()
    for t in peers:
        remote(k_ref.at[t % 2, :, cols(t // 2)], kbuf.at[s], K_SEM, (g, t))
    pltpu.make_async_copy(k_ref.at[core, :, cols(s // 2)], kbuf.at[s], recv_sem.at[K_SEM]).start()

    q_copy.wait()

    def send_head(h, c):
        pltpu.make_async_copy(
            q_ref.at[core, :, cols((s // 2) * HEADS + h)], qbuf.at[h, s], recv_sem.at[Q_SEM + h]
        ).start()
        for t in peers:
            remote(q_ref.at[t % 2, :, cols((t // 2) * HEADS + h)], qbuf.at[h, s], Q_SEM + h, (g, t))
        return c

    lax.fori_loop(0, HEADS, send_head, 0)
    v_copy.wait()
    pltpu.make_async_copy(v_ref.at[core, :, cols(s // 2)], vbuf.at[s], recv_sem.at[V_SEM]).start()
    for t in peers:
        remote(v_ref.at[t % 2, :, cols(t // 2)], vbuf.at[s], V_SEM, (g, t))

    wt_copy.wait()
    remote(wbuf.at[core], wbuf.at[core], W_SEM, sibling)

    def wait_all(ref, sem):
        pltpu.make_async_copy(ref, ref, sem).wait()

    len0 = len_ref[0]
    len1 = len_ref[1]

    hid_copy.wait()
    place = s * TOK + lax.broadcasted_iota(jnp.int32, (16, TOK), 1)
    ones = jnp.ones((16, TOK), F32)
    zeros = jnp.zeros((16, TOK), F32)
    for doc, length in ((0, len0), (1, len1)):
        mask = jnp.where(place < length, ones, zeros).astype(BF16)
        inv_len = jnp.full((1, 1), 1.0, F32) / jnp.full((1, 1), length, jnp.int32).astype(F32)

        part = jnp.dot(mask, hbuf[doc], preferred_element_type=F32)[0:1] * inv_len
        for t in range(RANKS):
            resid[t, doc:doc + 1, :] = part[:, 256 * t:256 * t + LANES]
            resid[t, 2 + doc:3 + doc, :] = part[:, 256 * t + LANES:256 * t + 256]

    my_len = len_ref[core]

    wait_all(kbuf, recv_sem.at[K_SEM])

    def one_head(h, c):
        signal(sync.at[h], z_next, z_prev)
        wait_all(qbuf.at[h], recv_sem.at[Q_SEM + h])
        for i in range(LEN // QB):
            n = (i + 1) * QB
            nb = n // TOK
            keys = kbuf[0:nb].reshape(n, LANES)
            queries = qbuf[h, 2 * i:2 * i + 2].reshape(QB, LANES)
            sref = sbuf.at[i % 2]
            sref[0:n, :] = lax.dot_general(
                keys, queries, (((1,), (1,)), ((), ())), preferred_element_type=F32)
            diag = sref[n - QB:n, :]
            vis = lax.broadcasted_iota(jnp.int32, (QB, QB), 0) <= lax.broadcasted_iota(
                jnp.int32, (QB, QB), 1)
            sref[n - QB:n, :] = jnp.where(vis, diag, -1e30)
            peak = sref[0:8, :]
            for r in range(8, n, 8):
                peak = jnp.maximum(peak, sref[r:r + 8, :])
            peak = jnp.max(peak, axis=0, keepdims=True)
            total = jnp.zeros((8, QB), F32)
            step = 64
            for r in range(0, n, step):
                e = jnp.exp2((sref[r:r + step, :] - peak) * EXP2_SCALE)
                sref[r:r + step, :] = e
                total = total + jnp.sum(e.reshape(step // 8, 8, QB), axis=0)
            total = jnp.sum(total, axis=0, keepdims=True)
            t_at = i * QB + lax.broadcasted_iota(jnp.int32, (1, QB), 1)
            ratio = jnp.where(t_at < my_len, 1.0 / total, 0.0)
            for r in range(0, n, step):
                e = sref[r:r + step, :] * ratio
                e = e[:, 0:LANES] + e[:, LANES:]
                if r >= n - QB:
                    wsum[r:r + step, :] = e
                else:
                    wsum[r:r + step, :] += e
        lane_ones = jnp.ones((8, LANES), F32)
        w_row = lax.dot_general(
            lane_ones, wsum[...], (((1,), (1,)), ((), ())), precision=HIGHEST,
            preferred_element_type=F32)
        for p, part in enumerate(split3(w_row[0:1])):
            lhs_ref[pl.ds(p * HEADS + h, 1), :] = part
        pl.semaphore_wait(sync.at[h], 2)
        return c

    lhs_ref[12:16, :] = jnp.zeros((4, LEN), F32)
    lax.fori_loop(0, HEADS, one_head, 0)
    signal(sync.at[HEADS], far_half)
    lhs = lhs_ref[...].astype(BF16)

    wait_all(vbuf, recv_sem.at[V_SEM])
    inv_my_len = jnp.full((1, 1), 1.0, F32) / jnp.full((1, 1), my_len, jnp.int32).astype(F32)
    out = jnp.dot(lhs, vbuf[...].reshape(LEN, LANES), preferred_element_type=F32)
    mine = (out[0:4] + out[4:8] + out[8:12]) * inv_my_len

    pl.semaphore_wait(sync.at[HEADS], 1)

    wide_mine = jnp.concatenate([mine[h:h + 1] for h in range(HEADS)], axis=1)
    lhs2 = jnp.concatenate(
        list(split3(wide_mine)) + [jnp.zeros((13, HEADS * LANES), F32)], axis=0).astype(BF16)
    wait_all(wbuf.at[0], recv_sem.at[W_SEM])
    tile_row = lax.broadcasted_iota(jnp.int32, (4, LANES), 0)

    for dy in (1, 0):
        part = jnp.dot(
            lhs2,
            wbuf[:, :, pl.ds(pl.multiple_of(rows[dy] * 256, 2048), 2048)].reshape(
                HEADS * LANES, 2048),
            preferred_element_type=F32)
        part = part[0:1] + part[1:2] + part[2:3]
        for k in range(8):
            rs_out[rows[dy] + k] = resid[rows[dy] + k] + jnp.where(
                tile_row == core, part[:, 256 * k:256 * k + LANES],
                jnp.where(tile_row == 2 + core, part[:, 256 * k + LANES:256 * k + 256], 0.0))
        for dx in (2, 1, 3, 0):
            for dc in (1, 0):
                t = at(dy, dx, dc)
                mine_there = rs_buf.at[y_hi * RANKS + s]
                remote(rs_out.at[t], mine_there, RS_SEM, (z * 2 + 1 - y_hi, t))
                if dy or dx or dc:
                    remote(rs_out.at[t], mine_there, RS_SEM, (g, t))
    rs_buf[y_hi * RANKS + s] = rs_out[s]

    sib[core] = mine
    remote(sib.at[core], sib.at[core], SIB_SEM, sibling)

    wait_all(rs_buf.at[pl.ds(0, 2 * RANKS - 1)], recv_sem.at[RS_SEM])
    for half in range(2):
        raw = jnp.sum(rs_buf[half * RANKS:(half + 1) * RANKS], axis=0)
        rtile[half] = raw
        rg_buf[z, half] = raw

    for dz in (4, 3, 5, 2, 6, 1, 7):
        remote(rtile, rg_buf.at[z], RG_SEM, (((z + dz) % 8) * 2 + y_hi, s))

    @pl.when(s == g)
    def _():
        tg_buf[g] = rtile[y_hi]

    def send_cols(e, c):
        @pl.when(jnp.logical_or(s != g, e != s))
        def _():
            remote(rtile.at[y_hi], tg_buf.at[g], TG_SEM, (s, e))
        return c

    lax.fori_loop(0, RANKS, send_cols, 0)

    wait_all(sib.at[0], recv_sem.at[SIB_SEM])
    low = core == 0
    doc0 = jnp.where(low, sib[0, 0:2, :], sib[0, 2:4, :])
    doc1 = jnp.where(low, sib[1, 0:2, :], sib[1, 2:4, :])
    both = jnp.concatenate([doc0[0:1], doc1[0:1], doc0[1:2], doc1[1:2]], axis=0)
    ptile[...] = both
    pg_buf[g] = both

    def send_pooled(e, c):
        remote(ptile, pg_buf.at[g], PG_SEM, (lax.rem(g + e + 1, RANKS), s))
        return c

    lax.fori_loop(0, RANKS - 1, send_pooled, 0)

    wait_all(rg_buf.at[pl.ds(0, 7)], recv_sem.at[RG_SEM])
    for d in range(RANKS):
        for half in range(2):
            piece = rg_buf[d // 2, d % 2, 2 * half:2 * half + 2, :]
            for rep in range(4):
                rg_mat[32 * rep + 2 * d:32 * rep + 2 * d + 2, half * LANES:(half + 1) * LANES] = piece
    wide = lax.dot_general(
        rg_mat[0:32, :], rg_mat[...], (((1,), (1,)), ((), ())), precision=HIGHEST,
        preferred_element_type=F32)
    lane_group = lax.broadcasted_iota(jnp.int32, (8, LANES), 1) // 32
    packed = jnp.zeros((8, LANES), F32)
    for p in range(4):
        packed = packed + jnp.where(lane_group == p, wide[8 * p:8 * p + 8], 0.0)
    gtile[...] = packed
    gram_buf[s] = packed

    for t in peers:
        remote(gtile, gram_buf.at[s], GRAM_SEM, (g, t))

    wait_all(pg_buf.at[pl.ds(0, RANKS - 1)], recv_sem.at[PG_SEM])
    for d in range(RANKS):
        for half in range(2):
            end_ref[2 * d:2 * d + 2, half * LANES:(half + 1) * LANES] = pg_buf[
                d, 2 * half:2 * half + 2, :]

    @pl.when(s == g)
    def _():
        wait_all(tg_buf.at[pl.ds(0, RANKS - 1)], recv_sem.at[TG_SEM])

    @pl.when(s != g)
    def _():
        wait_all(tg_buf, recv_sem.at[TG_SEM])

    for d in range(RANKS):
        for half in range(2):
            end_ref[32 + 2 * d:34 + 2 * d, half * LANES:(half + 1) * LANES] = tg_buf[
                d, 2 * half:2 * half + 2, :]

    wait_all(gram_buf.at[pl.ds(0, RANKS - 1)], recv_sem.at[GRAM_SEM])
    gp = jnp.sum(gram_buf[...], axis=0)
    end_ref[64:72, 0:LANES] = gp
    end_ref[64:72, LANES:] = gp

    some = RANKS - 1
    wait_all(kbuf.at[pl.ds(0, some)], send_sem.at[K_SEM])
    for h in range(HEADS):
        wait_all(qbuf.at[h, pl.ds(0, some)], send_sem.at[Q_SEM + h])
    wait_all(vbuf.at[pl.ds(0, some)], send_sem.at[V_SEM])
    wait_all(sib.at[0], send_sem.at[SIB_SEM])
    wait_all(wbuf.at[0], send_sem.at[W_SEM])
    wait_all(rs_buf.at[pl.ds(0, 2 * RANKS - 1)], send_sem.at[RS_SEM])
    wait_all(rg_buf.at[pl.ds(0, 7)], send_sem.at[RG_SEM])

    @pl.when(s == g)
    def _():
        wait_all(tg_buf.at[pl.ds(0, some)], send_sem.at[TG_SEM])

    @pl.when(s != g)
    def _():
        wait_all(tg_buf, send_sem.at[TG_SEM])

    wait_all(pg_buf.at[pl.ds(0, some)], send_sem.at[PG_SEM])
    wait_all(gram_buf.at[pl.ds(0, some)], send_sem.at[GRAM_SEM])


def finish(end_ref, pos_ref, cost_ref, wo_ref):
    g = lax.axis_index("dp")
    pooled = end_ref[0:32, :]
    raw = end_ref[32:64, :]
    gp = end_ref[64:72, 0:LANES]
    ri = lax.broadcasted_iota(jnp.int32, (32, 32), 0)
    ci = lax.broadcasted_iota(jnp.int32, (32, 32), 1)
    eye = ri == ci
    eye_f = jnp.where(eye, 1.0, 0.0)
    hot_t = jnp.where(ri == pos_ref[...], 1.0, 0.0)
    hot = lax.dot_general(
        eye_f, hot_t, (((1,), (1,)), ((), ())), precision=HIGHEST, preferred_element_type=F32)
    gram = jnp.concatenate(
        [gp if p == 0 else pltpu.roll(gp, LANES - 32 * p, 1) for p in range(4)], axis=0)[:, 0:32]
    on_diag = jnp.where(eye, gram, 0.0)
    sq_i = jnp.sum(on_diag, axis=1, keepdims=True) + EPS
    sq_j = jnp.sum(on_diag, axis=0, keepdims=True) + EPS
    inv_i = lax.rsqrt(sq_i)
    inv_j = lax.rsqrt(sq_j)
    sims = gram * inv_i * inv_j * INV_TEMP
    raised = jnp.where(eye, 0.0, jnp.exp(sims - INV_TEMP))
    tot_i = jnp.sum(raised, axis=1, keepdims=True)
    tot_j = jnp.sum(raised, axis=0, keepdims=True)
    cost = jnp.log(tot_i) + INV_TEMP - jnp.sum(sims * hot, axis=1, keepdims=True)
    both_grad = raised / tot_i + raised / tot_j - hot - hot_t
    weighted = both_grad * inv_j * INV_TEMP
    along = jnp.sum(weighted * gram, axis=1, keepdims=True)
    coef = inv_i * weighted - eye_f * (inv_i * along / sq_i)
    grad_raw = jnp.dot(coef, raw, precision=HIGHEST, preferred_element_type=F32)
    ph, pm, pl_ = split3(pooled)
    gh, gm, gl = split3(grad_raw)
    left = jnp.concatenate([ph, ph, pm, pm, ph, pl_], axis=0).astype(BF16)
    right = jnp.concatenate([gh, gm, gh, gm, gl, gh], axis=0).astype(BF16)
    wo_ref[...] = lax.dot_general(
        left, right, (((0,), (0,)), ((), ())), preferred_element_type=F32)
    doc_at = lax.broadcasted_iota(jnp.int32, (32, 1), 0)
    cost_ref[0] = jnp.sum(jnp.where(doc_at == 2 * g, cost, 0.0))
    cost_ref[1] = jnp.sum(jnp.where(doc_at == 2 * g + 1, cost, 0.0))


def shards(q_proj, k_proj, v_proj, hidden_in, out_weight, doc_lengths, positive):
    any_spec = pl.BlockSpec(memory_space=pltpu.HBM)
    smem = pl.BlockSpec(memory_space=pltpu.SMEM)
    vmem = pl.BlockSpec(memory_space=pltpu.VMEM)
    tile = (RANKS, 4, LANES)
    end = pl.pallas_call(
        kernel,
        out_shape=jax.ShapeDtypeStruct((72, 256), F32),
        in_specs=[any_spec] * 5 + [smem],
        out_specs=vmem,
        scratch_shapes=[
            pltpu.VMEM((2, TOK, 4096), BF16),
            pltpu.VMEM((2, TOK, 1024), BF16),
            pltpu.VMEM((2, TOK, 1024), BF16),
            pltpu.VMEM((HEADS, RANKS, TOK, LANES), BF16),
            pltpu.VMEM((RANKS, TOK, LANES), BF16),
            pltpu.VMEM((RANKS, TOK, LANES), BF16),
            pltpu.VMEM((2, TOK, 4096), BF16),
            pltpu.VMEM((2, 256, 4096), BF16),
            pltpu.VMEM((2, LEN, QB), F32),
            pltpu.VMEM((LEN, LANES), F32),
            pltpu.VMEM(tile, F32),
            pltpu.VMEM((2, 4, LANES), F32),
            pltpu.VMEM(tile, F32),
            pltpu.VMEM((2 * RANKS, 4, LANES), F32),
            pltpu.VMEM((2, 4, LANES), F32),
            pltpu.VMEM((8, 2, 4, LANES), F32),
            pltpu.VMEM(tile, F32),
            pltpu.VMEM((4, LANES), F32),
            pltpu.VMEM(tile, F32),
            pltpu.VMEM((8, LANES), F32),
            pltpu.VMEM((RANKS, 8, LANES), F32),
            pltpu.VMEM((16, LEN), F32),
            pltpu.VMEM((128, 256), F32),
            pltpu.SemaphoreType.DMA((N_SEM,)),
            pltpu.SemaphoreType.DMA((N_SEM,)),
            pltpu.SemaphoreType.REGULAR((5,)),
        ],
        compiler_params=pltpu.CompilerParams(
            collective_id=0, has_side_effects=True, vmem_limit_bytes=107 * 2**19),
    )(q_proj, k_proj, v_proj, hidden_in, out_weight, doc_lengths)
    return pl.pallas_call(
        finish,
        out_shape=(
            jax.ShapeDtypeStruct((2,), F32),
            jax.ShapeDtypeStruct((256, 256), F32),
        ),
        in_specs=[vmem] * 2,
        out_specs=(smem, vmem),
        compiler_params=pltpu.CompilerParams(vmem_limit_bytes=107 * 2**19),
    )(end, positive.reshape(1, 32))


def solution(mesh):
    return jax.shard_map(
        shards,
        mesh=mesh,
        in_specs=(
            P("dp", "seq", None),
            P("dp", "seq", None),
            P("dp", "seq", None),
            P("dp", "seq", None),
            P("seq", None),
            P("dp"),
            P(),
        ),
        out_specs=(P("dp"), P("seq", "dp")),
        check_vma=False,
    )
```

```python
import math

import jax
import jax.numpy as jnp
from jax import lax
from jax.experimental import pallas as pl
from jax.experimental.pallas import tpu as pltpu
from jax.sharding import PartitionSpec as P

MESH = pl.DeviceIdType.MESH
F32 = jnp.float32
BF16 = jnp.bfloat16
HIGHEST = lax.Precision.HIGHEST
LANES = 128
TOK = 128
RANKS = 16
HEADS = 4
LEN = 2048
QB = 256
EXP2_SCALE = math.log2(math.e) / math.sqrt(128.0)
INV_TEMP = 20.0
EPS = 1e-06

(K_SEM, Q_SEM, V_SEM, SIB_SEM, RS_SEM, RG_SEM, TG_SEM, PG_SEM, GRAM_SEM, HID_SEM, W_SEM,
 K_IN_SEM, Q_IN_SEM, V_IN_SEM, W_IN_SEM) = (0, 1, 5, 6, 7, 8, 9, 10, 11, 12, 13, 14, 15, 16, 17)
N_SEM = 18


def split3(x):
    hi = x.astype(BF16).astype(F32)
    mid = (x - hi).astype(BF16).astype(F32)
    lo = x - hi - mid
    return hi, mid, lo


def kernel(
    q_hbm, k_hbm, v_hbm, hid_ref, wt_ref, len_ref,
    end_ref,
    q_ref, k_ref, v_ref, qbuf, kbuf, vbuf, hbuf, wbuf, sbuf, wsum, resid,
    sib, rs_out, rs_buf, rtile, rg_buf, tg_buf, ptile, pg_buf, gtile, gram_buf,
    lhs_ref, rg_mat,
    send_sem, recv_sem, sync,
):
    g = lax.axis_index("dp")
    s = lax.axis_index("seq")
    core = s % 2
    col = (s // 2) % 4
    row = s // 8

    rows = [row * 8, (1 - row) * 8]
    ring = [((col + dx) % 4) * 2 for dx in range(4)]
    cores = [core, 1 - core]

    def at(dy, dx, dc):
        return rows[dy] + ring[dx] + cores[dc]

    peers = []
    for dc in range(2):
        for dx in (2, 1, 0, 3):
            peers.append(at(1, dx, dc))
            if dc or dx != 2:
                peers.append(at(0, (dx + 2) % 4, dc))

    z = g // 2
    y_hi = g % 2
    sibling = (g, s + 1 - 2 * core)
    z_next = (((z + 1) % 8) * 2 + y_hi, s)
    z_prev = (((z + 7) % 8) * 2 + y_hi, s)
    far_half = (z * 2 + 1 - y_hi, s)

    def signal(sem, *targets):
        for target in targets:
            pl.semaphore_signal(sem, inc=1, device_id=target, device_id_type=MESH)

    barrier = pltpu.get_barrier_semaphore()
    for t in peers:
        signal(barrier, (g, t))
    signal(barrier, far_half, z_next, z_prev)

    k_copy = pltpu.make_async_copy(k_hbm, k_ref, recv_sem.at[K_IN_SEM])
    k_copy.start()
    q_copy = pltpu.make_async_copy(q_hbm, q_ref, recv_sem.at[Q_IN_SEM])
    q_copy.start()
    v_copy = pltpu.make_async_copy(v_hbm, v_ref, recv_sem.at[V_IN_SEM])
    v_copy.start()
    hid_copy = pltpu.make_async_copy(hid_ref, hbuf, recv_sem.at[HID_SEM])
    hid_copy.start()
    wt_copy = pltpu.make_async_copy(wt_ref, wbuf.at[core], recv_sem.at[W_IN_SEM])
    wt_copy.start()

    pl.semaphore_wait(barrier, RANKS + 2)

    def remote(src, dst, sem, target):
        pltpu.make_async_remote_copy(
            src_ref=src, dst_ref=dst, send_sem=send_sem.at[sem], recv_sem=recv_sem.at[sem],
            device_id=target, device_id_type=MESH,
        ).start()

    def cols(first):
        return pl.ds(pl.multiple_of(first * LANES, LANES), LANES)

    k_copy.wait()
    for t in peers:
        remote(k_ref.at[t % 2, :, cols(t // 2)], kbuf.at[s], K_SEM, (g, t))
    pltpu.make_async_copy(k_ref.at[core, :, cols(s // 2)], kbuf.at[s], recv_sem.at[K_SEM]).start()

    q_copy.wait()

    def send_head(h, c):
        pltpu.make_async_copy(
            q_ref.at[core, :, cols((s // 2) * HEADS + h)], qbuf.at[h, s], recv_sem.at[Q_SEM + h]
        ).start()
        for t in peers:
            remote(q_ref.at[t % 2, :, cols((t // 2) * HEADS + h)], qbuf.at[h, s], Q_SEM + h, (g, t))
        return c

    lax.fori_loop(0, HEADS, send_head, 0)
    v_copy.wait()
    pltpu.make_async_copy(v_ref.at[core, :, cols(s // 2)], vbuf.at[s], recv_sem.at[V_SEM]).start()
    for t in peers:
        remote(v_ref.at[t % 2, :, cols(t // 2)], vbuf.at[s], V_SEM, (g, t))

    wt_copy.wait()
    remote(wbuf.at[core], wbuf.at[core], W_SEM, sibling)

    def wait_all(ref, sem):
        pltpu.make_async_copy(ref, ref, sem).wait()

    len0 = len_ref[0]
    len1 = len_ref[1]

    hid_copy.wait()
    place = s * TOK + lax.broadcasted_iota(jnp.int32, (16, TOK), 1)
    ones = jnp.ones((16, TOK), F32)
    zeros = jnp.zeros((16, TOK), F32)
    for doc, length in ((0, len0), (1, len1)):
        mask = jnp.where(place < length, ones, zeros).astype(BF16)
        inv_len = jnp.full((1, 1), 1.0, F32) / jnp.full((1, 1), length, jnp.int32).astype(F32)

        part = jnp.dot(mask, hbuf[doc], preferred_element_type=F32)[0:1] * inv_len
        for t in range(RANKS):
            resid[t, doc:doc + 1, :] = part[:, 256 * t:256 * t + LANES]
            resid[t, 2 + doc:3 + doc, :] = part[:, 256 * t + LANES:256 * t + 256]

    my_len = len_ref[core]

    wait_all(kbuf, recv_sem.at[K_SEM])

    def one_head(h, c):
        signal(sync.at[h], z_next, z_prev)
        wait_all(qbuf.at[h], recv_sem.at[Q_SEM + h])
        for i in range(LEN // QB):
            n = (i + 1) * QB
            nb = n // TOK
            keys = kbuf[0:nb].reshape(n, LANES)
            queries = qbuf[h, 2 * i:2 * i + 2].reshape(QB, LANES)
            sref = sbuf.at[i % 2]
            sref[0:n, :] = lax.dot_general(
                keys, queries, (((1,), (1,)), ((), ())), preferred_element_type=F32)
            diag = sref[n - QB:n, :]
            vis = lax.broadcasted_iota(jnp.int32, (QB, QB), 0) <= lax.broadcasted_iota(
                jnp.int32, (QB, QB), 1)
            sref[n - QB:n, :] = jnp.where(vis, diag, -1e30)
            peak = sref[0:8, :]
            for r in range(8, n, 8):
                peak = jnp.maximum(peak, sref[r:r + 8, :])
            peak = jnp.max(peak, axis=0, keepdims=True)
            total = jnp.zeros((8, QB), F32)
            step = 64
            for r in range(0, n, step):
                e = jnp.exp2((sref[r:r + step, :] - peak) * EXP2_SCALE)
                sref[r:r + step, :] = e
                total = total + jnp.sum(e.reshape(step // 8, 8, QB), axis=0)
            total = jnp.sum(total, axis=0, keepdims=True)
            t_at = i * QB + lax.broadcasted_iota(jnp.int32, (1, QB), 1)
            ratio = jnp.where(t_at < my_len, 1.0 / total, 0.0)
            for r in range(0, n, step):
                e = sref[r:r + step, :] * ratio
                e = e[:, 0:LANES] + e[:, LANES:]
                if r >= n - QB:
                    wsum[r:r + step, :] = e
                else:
                    wsum[r:r + step, :] += e
        lane_ones = jnp.ones((8, LANES), F32)
        w_row = lax.dot_general(
            lane_ones, wsum[...], (((1,), (1,)), ((), ())), precision=HIGHEST,
            preferred_element_type=F32)
        for p, part in enumerate(split3(w_row[0:1])):
            lhs_ref[pl.ds(p * HEADS + h, 1), :] = part
        pl.semaphore_wait(sync.at[h], 2)
        return c

    lhs_ref[12:16, :] = jnp.zeros((4, LEN), F32)
    lax.fori_loop(0, HEADS, one_head, 0)
    signal(sync.at[HEADS], far_half)
    lhs = lhs_ref[...].astype(BF16)

    wait_all(vbuf, recv_sem.at[V_SEM])
    inv_my_len = jnp.full((1, 1), 1.0, F32) / jnp.full((1, 1), my_len, jnp.int32).astype(F32)
    out = jnp.dot(lhs, vbuf[...].reshape(LEN, LANES), preferred_element_type=F32)
    mine = (out[0:4] + out[4:8] + out[8:12]) * inv_my_len

    pl.semaphore_wait(sync.at[HEADS], 1)

    wide_mine = jnp.concatenate([mine[h:h + 1] for h in range(HEADS)], axis=1)
    lhs2 = jnp.concatenate(
        list(split3(wide_mine)) + [jnp.zeros((13, HEADS * LANES), F32)], axis=0).astype(BF16)
    wait_all(wbuf.at[0], recv_sem.at[W_SEM])
    tile_row = lax.broadcasted_iota(jnp.int32, (4, LANES), 0)

    for dy in (1, 0):
        part = jnp.dot(
            lhs2,
            wbuf[:, :, pl.ds(pl.multiple_of(rows[dy] * 256, 2048), 2048)].reshape(
                HEADS * LANES, 2048),
            preferred_element_type=F32)
        part = part[0:1] + part[1:2] + part[2:3]
        for k in range(8):
            rs_out[rows[dy] + k] = resid[rows[dy] + k] + jnp.where(
                tile_row == core, part[:, 256 * k:256 * k + LANES],
                jnp.where(tile_row == 2 + core, part[:, 256 * k + LANES:256 * k + 256], 0.0))
        for dx in (2, 1, 3, 0):
            for dc in (1, 0):
                t = at(dy, dx, dc)
                mine_there = rs_buf.at[y_hi * RANKS + s]
                remote(rs_out.at[t], mine_there, RS_SEM, (z * 2 + 1 - y_hi, t))
                if dy or dx or dc:
                    remote(rs_out.at[t], mine_there, RS_SEM, (g, t))
    rs_buf[y_hi * RANKS + s] = rs_out[s]

    sib[core] = mine
    remote(sib.at[core], sib.at[core], SIB_SEM, sibling)

    wait_all(rs_buf.at[pl.ds(0, 2 * RANKS - 1)], recv_sem.at[RS_SEM])
    for half in range(2):
        raw = jnp.sum(rs_buf[half * RANKS:(half + 1) * RANKS], axis=0)
        rtile[half] = raw
        rg_buf[z, half] = raw

    for dz in (4, 3, 5, 2, 6, 1, 7):
        remote(rtile, rg_buf.at[z], RG_SEM, (((z + dz) % 8) * 2 + y_hi, s))

    @pl.when(s == g)
    def _():
        tg_buf[g] = rtile[y_hi]

    def send_cols(e, c):
        @pl.when(jnp.logical_or(s != g, e != s))
        def _():
            remote(rtile.at[y_hi], tg_buf.at[g], TG_SEM, (s, e))
        return c

    lax.fori_loop(0, RANKS, send_cols, 0)

    wait_all(sib.at[0], recv_sem.at[SIB_SEM])
    low = core == 0
    doc0 = jnp.where(low, sib[0, 0:2, :], sib[0, 2:4, :])
    doc1 = jnp.where(low, sib[1, 0:2, :], sib[1, 2:4, :])
    both = jnp.concatenate([doc0[0:1], doc1[0:1], doc0[1:2], doc1[1:2]], axis=0)
    ptile[...] = both
    pg_buf[g] = both

    def send_pooled(e, c):
        remote(ptile, pg_buf.at[g], PG_SEM, (lax.rem(g + e + 1, RANKS), s))
        return c

    lax.fori_loop(0, RANKS - 1, send_pooled, 0)

    wait_all(rg_buf.at[pl.ds(0, 7)], recv_sem.at[RG_SEM])
    for d in range(RANKS):
        for half in range(2):
            piece = rg_buf[d // 2, d % 2, 2 * half:2 * half + 2, :]
            rg_mat[2 * d:2 * d + 2, half * LANES:(half + 1) * LANES] = piece
    for rep in range(1, 4):
        rg_mat[32 * rep:32 * rep + 32, :] = rg_mat[0:32, :]
    wide = lax.dot_general(
        rg_mat[0:32, :], rg_mat[...], (((1,), (1,)), ((), ())), precision=HIGHEST,
        preferred_element_type=F32)
    lane_group = lax.broadcasted_iota(jnp.int32, (8, LANES), 1) // 32
    packed = jnp.zeros((8, LANES), F32)
    for p in range(4):
        packed = packed + jnp.where(lane_group == p, wide[8 * p:8 * p + 8], 0.0)
    gtile[...] = packed
    gram_buf[s] = packed

    for t in peers:
        remote(gtile, gram_buf.at[s], GRAM_SEM, (g, t))

    wait_all(pg_buf.at[pl.ds(0, RANKS - 1)], recv_sem.at[PG_SEM])
    for d in range(RANKS):
        for half in range(2):
            end_ref[2 * d:2 * d + 2, half * LANES:(half + 1) * LANES] = pg_buf[
                d, 2 * half:2 * half + 2, :]

    @pl.when(s == g)
    def _():
        wait_all(tg_buf.at[pl.ds(0, RANKS - 1)], recv_sem.at[TG_SEM])

    @pl.when(s != g)
    def _():
        wait_all(tg_buf, recv_sem.at[TG_SEM])

    for d in range(RANKS):
        for half in range(2):
            end_ref[32 + 2 * d:34 + 2 * d, half * LANES:(half + 1) * LANES] = tg_buf[
                d, 2 * half:2 * half + 2, :]

    some = RANKS - 1
    wait_all(kbuf.at[pl.ds(0, some)], send_sem.at[K_SEM])
    for h in range(HEADS):
        wait_all(qbuf.at[h, pl.ds(0, some)], send_sem.at[Q_SEM + h])
    wait_all(vbuf.at[pl.ds(0, some)], send_sem.at[V_SEM])
    wait_all(sib.at[0], send_sem.at[SIB_SEM])
    wait_all(wbuf.at[0], send_sem.at[W_SEM])
    wait_all(rs_buf.at[pl.ds(0, 2 * RANKS - 1)], send_sem.at[RS_SEM])
    wait_all(rg_buf.at[pl.ds(0, 7)], send_sem.at[RG_SEM])

    @pl.when(s == g)
    def _():
        wait_all(tg_buf.at[pl.ds(0, some)], send_sem.at[TG_SEM])

    @pl.when(s != g)
    def _():
        wait_all(tg_buf, send_sem.at[TG_SEM])

    wait_all(pg_buf.at[pl.ds(0, some)], send_sem.at[PG_SEM])

    wait_all(gram_buf.at[pl.ds(0, RANKS - 1)], recv_sem.at[GRAM_SEM])
    gp = jnp.sum(gram_buf[...], axis=0)
    end_ref[64:72, 0:LANES] = gp
    end_ref[64:72, LANES:] = gp

    wait_all(gram_buf.at[pl.ds(0, RANKS - 1)], send_sem.at[GRAM_SEM])


def finish(end_ref, pos_ref, cost_ref, wo_ref):
    g = lax.axis_index("dp")
    pooled = end_ref[0:32, :]
    raw = end_ref[32:64, :]
    gp = end_ref[64:72, 0:LANES]
    ri = lax.broadcasted_iota(jnp.int32, (32, 32), 0)
    ci = lax.broadcasted_iota(jnp.int32, (32, 32), 1)
    eye = ri == ci
    eye_f = jnp.where(eye, 1.0, 0.0)
    hot_t = jnp.where(ri == pos_ref[...], 1.0, 0.0)
    hot = lax.dot_general(
        eye_f, hot_t, (((1,), (1,)), ((), ())), precision=HIGHEST, preferred_element_type=F32)
    gram = jnp.concatenate(
        [gp if p == 0 else pltpu.roll(gp, LANES - 32 * p, 1) for p in range(4)], axis=0)[:, 0:32]
    on_diag = jnp.where(eye, gram, 0.0)
    sq_i = jnp.sum(on_diag, axis=1, keepdims=True) + EPS
    sq_j = jnp.sum(on_diag, axis=0, keepdims=True) + EPS
    inv_i = lax.rsqrt(sq_i)
    inv_j = lax.rsqrt(sq_j)
    sims = gram * inv_i * inv_j * INV_TEMP
    raised = jnp.where(eye, 0.0, jnp.exp(sims - INV_TEMP))
    tot_i = jnp.sum(raised, axis=1, keepdims=True)
    tot_j = jnp.sum(raised, axis=0, keepdims=True)
    cost = jnp.log(tot_i) + INV_TEMP - jnp.sum(sims * hot, axis=1, keepdims=True)
    both_grad = raised / tot_i + raised / tot_j - hot - hot_t
    weighted = both_grad * inv_j * INV_TEMP
    along = jnp.sum(weighted * gram, axis=1, keepdims=True)
    coef = inv_i * weighted - eye_f * (inv_i * along / sq_i)
    grad_raw = jnp.dot(coef, raw, precision=HIGHEST, preferred_element_type=F32)
    ph, pm, pl_ = split3(pooled)
    gh, gm, gl = split3(grad_raw)
    left = jnp.concatenate([ph, ph, pm, pm, ph, pl_], axis=0).astype(BF16)
    right = jnp.concatenate([gh, gm, gh, gm, gl, gh], axis=0).astype(BF16)
    wo_ref[...] = lax.dot_general(
        left, right, (((0,), (0,)), ((), ())), preferred_element_type=F32)
    doc_at = lax.broadcasted_iota(jnp.int32, (32, 1), 0)
    cost_ref[0] = jnp.sum(jnp.where(doc_at == 2 * g, cost, 0.0))
    cost_ref[1] = jnp.sum(jnp.where(doc_at == 2 * g + 1, cost, 0.0))


def shards(q_proj, k_proj, v_proj, hidden_in, out_weight, doc_lengths, positive):
    any_spec = pl.BlockSpec(memory_space=pltpu.HBM)
    smem = pl.BlockSpec(memory_space=pltpu.SMEM)
    vmem = pl.BlockSpec(memory_space=pltpu.VMEM)
    tile = (RANKS, 4, LANES)
    end = pl.pallas_call(
        kernel,
        out_shape=jax.ShapeDtypeStruct((72, 256), F32),
        in_specs=[any_spec] * 5 + [smem],
        out_specs=vmem,
        scratch_shapes=[
            pltpu.VMEM((2, TOK, 4096), BF16),
            pltpu.VMEM((2, TOK, 1024), BF16),
            pltpu.VMEM((2, TOK, 1024), BF16),
            pltpu.VMEM((HEADS, RANKS, TOK, LANES), BF16),
            pltpu.VMEM((RANKS, TOK, LANES), BF16),
            pltpu.VMEM((RANKS, TOK, LANES), BF16),
            pltpu.VMEM((2, TOK, 4096), BF16),
            pltpu.VMEM((2, 256, 4096), BF16),
            pltpu.VMEM((2, LEN, QB), F32),
            pltpu.VMEM((LEN, LANES), F32),
            pltpu.VMEM(tile, F32),
            pltpu.VMEM((2, 4, LANES), F32),
            pltpu.VMEM(tile, F32),
            pltpu.VMEM((2 * RANKS, 4, LANES), F32),
            pltpu.VMEM((2, 4, LANES), F32),
            pltpu.VMEM((8, 2, 4, LANES), F32),
            pltpu.VMEM(tile, F32),
            pltpu.VMEM((4, LANES), F32),
            pltpu.VMEM(tile, F32),
            pltpu.VMEM((8, LANES), F32),
            pltpu.VMEM((RANKS, 8, LANES), F32),
            pltpu.VMEM((16, LEN), F32),
            pltpu.VMEM((128, 256), F32),
            pltpu.SemaphoreType.DMA((N_SEM,)),
            pltpu.SemaphoreType.DMA((N_SEM,)),
            pltpu.SemaphoreType.REGULAR((5,)),
        ],
        compiler_params=pltpu.CompilerParams(
            collective_id=0, has_side_effects=True, vmem_limit_bytes=107 * 2**19),
    )(q_proj, k_proj, v_proj, hidden_in, out_weight, doc_lengths)
    return pl.pallas_call(
        finish,
        out_shape=(
            jax.ShapeDtypeStruct((2,), F32),
            jax.ShapeDtypeStruct((256, 256), F32),
        ),
        in_specs=[vmem] * 2,
        out_specs=(smem, vmem),
        compiler_params=pltpu.CompilerParams(vmem_limit_bytes=107 * 2**19),
    )(end, positive.reshape(1, 32))


def solution(mesh):
    return jax.shard_map(
        shards,
        mesh=mesh,
        in_specs=(
            P("dp", "seq", None),
            P("dp", "seq", None),
            P("dp", "seq", None),
            P("dp", "seq", None),
            P("seq", None),
            P("dp"),
            P(),
        ),
        out_specs=(P("dp"), P("seq", "dp")),
        check_vma=False,
    )
```
